256 devices in a mesh: comp: 2 (over core), blk: 32 (over z, x), sub: 4 (over y).
Axes of the slice: x: 4, y: 4, z: 8, core: 2. Of those that a mesh axis runs over, the one named last changes fastest.
Arguments:
- state: float32 [2, 4, 80, 262144], P('comp', None, None, ('blk', 'sub')), may hold values from -6 to 6
- tile_ops: float32 [2, 2048, 128, 128], P('comp', ('blk', 'sub')), may hold values from -0.5 to 0.5
- kappa: float32 [2, 80, 262144], P('comp', None, ('blk', 'sub')), may hold values from 0.1 to 8
- active: int32 [2, 2048], P('comp', ('blk', 'sub')), may hold values from 2 to 80
- edge_local: int32 [2, 131072], P('comp', ('blk', 'sub')), may hold values from 0 to 2047
- edge_halo: int32 [2, 131072], P('comp', ('blk', 'sub')), may hold values from 0 to 1023
- edge_coef: float32 [2, 131072], P('comp', ('blk', 'sub')), may hold values from 0.25 to 2
- remap_src: int32 [2, 16384], P('comp', ('blk', 'sub')), may hold values from 0 to 15
- remap_owner: int32 [2, 16384, 1], P('comp', ('blk', 'sub')), may hold values from 0 to 127; in each aligned block of 128 rows (0 to 127, 128 to 255, ..., all dimensions but the last counted through in order) at most 2 rows name the same one
- remap_tile: int32 [2, 16384], P('comp', ('blk', 'sub')), may hold values from 0 to 15
- remap_weight: bfloat16 [2, 16384, 128, 128], P('comp', ('blk', 'sub')), may hold values from -0.1875 to 0.1875
Outputs:
- new_state: float32 [2, 4, 80, 262144], P('comp', None, None, ('blk', 'sub'))
- coupled_flux: float32 [2, 4, 262144], P('comp', None, ('blk', 'sub'))
The draws below stay inside these ranges and needn't reach their ends.
Inputs may be any that keep to these rules, and one draw needn't show every extreme that they name: `remap_owner`: within the 128 remap tiles of one device no owner is named more than 2 times, a bound that some block reaches.
All inputs are finite; a program needn't handle non-finite values.
Results may differ from the reference program's by a relative error of at most 0.0029.
Values sent between devices are 32-bit elements; how exact they have to be, the bound alone decides.
No kernel may reach another device: no remote copies, remote signals or barrier semaphores. Data moves between devices by JAX's collectives and lax.ppermute only.
A program may use at most 128 MiB of HBM per device.

```python
import math
import jax
import jax.numpy as jnp
import numpy as np
from jax import lax

COLS_DEV = 2048
TILE = 128
LEVELS = 80
FIELDS = 4
HALO_W = 512
REMAP_DEV = 128
TILES_DEV = 16
EDGES = 1024
CAP = 2
NCOLS = 262144
NTILES = 2048
NEDGES = 131072
NREMAP = 16384
N_BLK = 32
N_SUB = 4


def plant(result, rng, low, largest):
    longest = result.shape.index(max(result.shape))
    spots = []
    for shift in (0, 1):
        where = [jax.random.randint(jax.random.fold_in(rng, axis), (), 0, length) for axis, length in enumerate(result.shape)]
        where[longest] = (where[longest] + shift) % result.shape[longest]
        spots.append(tuple(where))
    return result.at[spots[0]].set(low).at[spots[1]].set(largest)


def block_scale(stream_key, dims, shards, low, high):
    def one(axis_at, blocks):
        steps = jax.random.uniform(jax.random.fold_in(jax.random.fold_in(stream_key, 6), axis_at), (blocks,), jnp.float32, low / len(shards), high / len(shards))
        return jnp.repeat(jnp.exp(steps), dims[axis_at] // blocks).reshape((-1,) + (1,) * (len(dims) - axis_at - 1))

    factor_of = one(*shards[0])
    for cut in shards[1:]:
        factor_of = factor_of * one(*cut)
    return factor_of


def deal_out(rng, own, number, rows, number_of, top, limit, slope):
    sequence = jax.random.permutation(rng, number_of)
    packed, ordinary = shares(number_of, rows * top, limit, slope, True), shares(number_of, rows * top, limit, slope, False)
    places = jnp.arange(number_of)

    def named(sizes, offset_by):
        used = int((sizes > 0).sum())
        fixed = max(1, used // 4)
        shifted = fixed + (places - fixed + offset_by * (used - fixed)) % max(1, number_of - fixed)
        return jnp.zeros((number_of,), jnp.int32).at[sequence[jnp.where(places < fixed, places, shifted)]].set(jnp.asarray(sizes, jnp.int32))

    sizes = jnp.where(number % 4 == 0, named(packed, number // 4), named(ordinary, number - number // 4 - 1))
    mixed = jax.random.permutation(jax.random.fold_in(own, 3), number_of)
    source_of, sink = mixed[0:number_of // 2 * 2:2], mixed[1:number_of // 2 * 2:2]
    margin = jnp.minimum(sizes[source_of] - 1, limit - sizes[sink]) // 2
    margin = jnp.where((source_of == sequence[0]) | (sink == sequence[0]) | (sizes[sink] == 0), 0, jnp.maximum(margin, 0))
    shifted = jax.random.randint(jax.random.fold_in(own, 4), (number_of // 2,), 0, 1 << 20) % (margin + 1)
    sizes = sizes.at[source_of].add(-shifted).at[sink].add(shifted)
    items = jnp.searchsorted(jnp.cumsum(sizes), jnp.arange(rows * top), side="right").astype(jnp.int32)
    listing = items.reshape(top, rows).T
    listing = listing[jax.random.permutation(jax.random.fold_in(own, 1), rows)]
    offset_by = jax.random.randint(jax.random.fold_in(own, 2), (rows, 1), 0, top)
    return jnp.take_along_axis(listing, (jnp.arange(top)[None, :] + offset_by) % top, axis=1)


def shares(count, total, bound, lean, full):
    weights = [(1 << 20) // math.isqrt(grade ** lean) + 1 for grade in range(1, count + 1)]
    largest = bound if full else min(bound, max(-(-total // count), total * weights[0] // sum(weights)))
    least = 1 if total - largest >= count - 1 else 0
    given, surplus = [largest] + [least] * (count - 1), total - largest - least * (count - 1)
    while surplus > 0:
        candidates = [i for i in range(1, count) if given[i] < largest] or [i for i in range(1, count) if given[i] < bound]
        pool, left = sum([weights[i] for i in candidates]), surplus
        for i in candidates:
            addition = min(bound - given[i], max(1, left * weights[i] // pool), surplus)
            given[i] = given[i] + addition
            surplus = surplus - addition
    return np.array(given)


def gaussian(rng, dims, spread, limit, shards=(), kind=jnp.bfloat16):
    array = spread * jax.random.normal(rng, dims, jnp.float32)
    if shards:
        array = array * block_scale(rng, dims, shards, -0.22, 0.18)
    return jnp.clip(array, -limit, limit).astype(kind)


def setup_inputs(seed: int = 0) -> dict:
    key_of = jax.random.split(jax.random.key(seed), 12)
    state = gaussian(key_of[0], (2, FIELDS, LEVELS, NCOLS), 1.0, 6.0, ((0, 2), (3, 128)), jnp.float32)
    tile_ops = gaussian(key_of[1], (2, NTILES, TILE, TILE), TILE ** -0.5, 0.5, ((0, 2), (1, 128)), jnp.float32)
    kappa = jnp.clip(jnp.exp(math.log(8.0) - 4.3820266 * jax.random.uniform(key_of[2], (2, LEVELS, NCOLS), jnp.float32) ** block_scale(key_of[2], (2, LEVELS, NCOLS), ((0, 2), (2, 128)), -0.2, 0.2)), 0.1, 8.0)
    active = plant(jax.random.randint(key_of[3], (2, NTILES), 2, LEVELS + 1), jax.random.fold_in(key_of[3], 1), 2, LEVELS).astype(jnp.int32)
    edge_local = plant(jax.random.randint(key_of[4], (2, NEDGES), 0, COLS_DEV), jax.random.fold_in(key_of[4], 1), 0, COLS_DEV - 1).astype(jnp.int32)
    edge_halo = plant(jax.random.randint(key_of[5], (2, NEDGES), 0, 2 * HALO_W), jax.random.fold_in(key_of[5], 1), 0, (2 * HALO_W) - 1).astype(jnp.int32)
    edge_coef = jnp.clip(jnp.exp(math.log(2.0) - 2.0794415 * jax.random.uniform(key_of[6], (2, NEDGES), jnp.float32) ** block_scale(key_of[6], (2, NEDGES), ((0, 2), (1, 128)), -0.2, 0.2)), 0.25, 2.0)
    remap_src = plant(jax.random.randint(key_of[7], (2, NREMAP), 0, TILES_DEV), jax.random.fold_in(key_of[7], 1), 0, TILES_DEV - 1).astype(jnp.int32)
    remap_owner_keys = jax.random.split(jax.random.fold_in(key_of[8], 1), 2 * NREMAP // REMAP_DEV)
    remap_owner_turns = jax.random.permutation(jax.random.fold_in(key_of[8], 3), 2 * NREMAP // REMAP_DEV)
    remap_owner = jax.vmap(lambda own, number: deal_out(jax.random.fold_in(key_of[8], 2), own, number, REMAP_DEV, N_BLK * N_SUB, 1, CAP, 2))(remap_owner_keys, remap_owner_turns).reshape((2, NREMAP, 1))
    remap_tile = plant(jax.random.randint(key_of[9], (2, NREMAP), 0, TILES_DEV), jax.random.fold_in(key_of[9], 1), 0, TILES_DEV - 1).astype(jnp.int32)
    remap_weight = gaussian(key_of[10], (2, NREMAP, TILE, TILE), (TILE * REMAP_DEV // TILES_DEV) ** -0.5, 0.1875, ((0, 2), (1, 128)))
    return {"state": state, "tile_ops": tile_ops, "kappa": kappa, "active": active, "edge_local": edge_local, "edge_halo": edge_halo, "edge_coef": edge_coef, "remap_src": remap_src, "remap_owner": remap_owner, "remap_tile": remap_tile, "remap_weight": remap_weight}


STEP = 0.25
RELAX = 0.5


def tile_apply(column_field, operators):
    rows = column_field.shape[0] * column_field.shape[1]
    blocks = column_field.reshape(rows, operators.shape[0], operators.shape[1])
    mixed = jnp.einsum("rtc,tcd->rtd", blocks, operators, precision=lax.Precision.HIGHEST)
    return mixed.reshape(column_field.shape)


def vertical_mix(column_field, diffusivity, active_cols):
    levels = column_field.shape[1]
    depth = jnp.arange(levels, dtype=jnp.int32)[:, None]
    inside = (depth < active_cols[None, :]).astype(jnp.float32)
    opened = (depth + 1 < active_cols[None, :]).astype(jnp.float32)
    upper = -STEP * diffusivity * opened
    lower = jnp.concatenate([jnp.zeros_like(upper[:1]), upper[:-1]], axis=0)
    diagonal = 1.0 - lower - upper
    ratios = []
    values = []
    for level in range(levels):
        if level == 0:
            pivot = diagonal[0]
            value_now = column_field[:, 0, :] / pivot
        else:
            pivot = diagonal[level] - lower[level] * ratios[-1]
            value_now = (column_field[:, level, :] - lower[level] * values[-1]) / pivot
        ratios.append(upper[level] / pivot)
        values.append(value_now)
    solved = [values[levels - 1]]
    for level in range(levels - 2, -1, -1):
        solved.append(values[level] - ratios[level] * solved[-1])
    solved = jnp.stack(solved[::-1], axis=1)
    return solved * inside[None]


def spread_tiles(counts, width):
    return jnp.broadcast_to(counts[:, None], (counts.shape[0], width)).reshape(-1)


def reference(state, tile_ops, kappa, active, edge_local, edge_halo, edge_coef, remap_src, remap_owner, remap_tile, remap_weight):
    group = N_BLK * N_SUB
    stars = []
    for comp_index in range(2):
        column_field = state[comp_index]
        tendency = tile_apply(column_field, tile_ops[comp_index])
        blocks = column_field.reshape(FIELDS, LEVELS, group, COLS_DEV)
        before = jnp.roll(blocks[..., COLS_DEV - HALO_W:], 1, axis=2)
        after = jnp.roll(blocks[..., :HALO_W], -1, axis=2)
        border = jnp.concatenate([before, after], axis=3)
        owners = jnp.arange(group, dtype=jnp.int32)[:, None]
        own_index = edge_local[comp_index].reshape(group, EDGES)
        remote_index = edge_halo[comp_index].reshape(group, EDGES)
        strength = edge_coef[comp_index].reshape(group, EDGES)
        remote = border[:, :, owners, remote_index]
        own_values = blocks[:, :, owners, own_index]
        exchange_flow = strength * (remote - own_values)
        extra = jnp.zeros_like(blocks).at[:, :, owners, own_index].add(exchange_flow)
        tendency = tendency + extra.reshape(column_field.shape)
        stars.append(column_field + STEP * tendency)
    fluxes = [None, None]
    for source in range(2):
        surface = stars[source][:, 0, :].astype(jnp.bfloat16).reshape(FIELDS, group, TILES_DEV, TILE)
        surface = jnp.transpose(surface, (1, 2, 0, 3))
        sources = remap_src[source].reshape(group, REMAP_DEV)
        weights = remap_weight[source].reshape(group, REMAP_DEV, TILE, TILE)

        def one_device(pieces):
            tiles_here, picked, matrices = pieces
            chosen = tiles_here[picked].astype(jnp.float32)
            return jnp.einsum("rfc,rcd->rfd", chosen, matrices.astype(jnp.float32), precision=lax.Precision.HIGHEST)

        products = lax.map(one_device, (surface, sources, weights))
        target = remap_owner[source][:, 0] * TILES_DEV + remap_tile[source]
        summed = jax.ops.segment_sum(products.reshape(group * REMAP_DEV, FIELDS, TILE), target, num_segments=group * TILES_DEV)
        fluxes[1 - source] = jnp.transpose(summed, (1, 0, 2)).reshape(FIELDS, group * COLS_DEV)
    outputs = []
    for comp_index in range(2):
        star = stars[comp_index]
        top_level = star[:, 0, :]
        star = star.at[:, 0, :].set(top_level + RELAX * (fluxes[comp_index] - top_level))
        active_cols = spread_tiles(active[comp_index], TILE)
        outputs.append(vertical_mix(star, kappa[comp_index], active_cols))
    return jnp.stack(outputs), jnp.stack(fluxes)
```

```python
import jax
import jax.numpy as jnp
from jax import lax
from jax.experimental import pallas as pl
from jax.experimental.pallas import tpu as pltpu
from jax.sharding import PartitionSpec as P

HALO_W = 512
LANES = 128
STEP = 0.25
RELAX = 0.5
CHUNK = 9
F32 = jnp.float32
BF16 = jnp.bfloat16
VMEM = pltpu.VMEM
SMEM = pltpu.SMEM


def split3(x):
    hi = x.astype(BF16)
    rest = x - hi.astype(F32)
    mid = rest.astype(BF16)
    low = (rest - mid.astype(F32)).astype(BF16)
    return hi, mid, low


def split2(x):
    hi = x.astype(BF16)
    return hi, (x - hi.astype(F32)).astype(BF16)


def mm(a, b):
    return jnp.dot(a, b, preferred_element_type=F32)


def vspec():
    return pl.BlockSpec(memory_space=VMEM)


def sspec():
    return pl.BlockSpec(memory_space=SMEM)


def hbm(x):
    return pltpu.with_memory_space_constraint(x, pltpu.HBM)


def aspec():
    return pl.BlockSpec(memory_space=pltpu.HBM)


def params(mib):
    return pltpu.CompilerParams(vmem_limit_bytes=mib * 1024 * 1024)


def sides(even_ref, columns):
    even = even_ref[0] == 1
    last = columns - HALO_W
    return [pl.multiple_of(jnp.where(even, *pair), LANES) for pair in ((last, 0), (0, last))]


def pack_top_body(even_ref, state_ref, one_ref, two_ref, window, sem):
    loads = [
        pltpu.make_async_copy(state_ref.at[0, :, pl.ds(0, 8), pl.ds(at, HALO_W)], window.at[i], sem.at[i])
        for i, at in enumerate(sides(even_ref, state_ref.shape[3]))
    ]
    for load in loads:
        load.start()
    for i, ref in enumerate((one_ref, two_ref)):
        loads[i].wait()
        ref[...] = window[i, :, 0, :]


def pack_top(even, state):
    fields = state.shape[1]
    return pl.pallas_call(
        pack_top_body,
        in_specs=[sspec(), aspec()],
        out_specs=[vspec()] * 2,
        out_shape=[jax.ShapeDtypeStruct((fields, HALO_W), F32)] * 2,
        scratch_shapes=[pltpu.VMEM((2, fields, 8, HALO_W), F32), pltpu.SemaphoreType.DMA((2,))],
        cost_estimate=pl.CostEstimate(flops=0, bytes_accessed=10**5, transcendentals=0),
    )(even, hbm(state))


def pack_body(even_ref, state_ref, _, one_ref, two_ref, sem):
    loads = [
        pltpu.make_async_copy(state_ref.at[0, :, :, pl.ds(at, HALO_W)], ref, sem.at[i])
        for i, (at, ref) in enumerate(zip(sides(even_ref, state_ref.shape[3]), (one_ref, two_ref)))
    ]
    for load in loads:
        load.start()
    for load in loads:
        load.wait()


def pack(even, state, after):
    _, fields, levels, _ = state.shape
    return pl.pallas_call(
        pack_body,
        in_specs=[sspec(), aspec(), pl.BlockSpec(memory_space=pl.ANY)],
        out_specs=[vspec()] * 2,
        out_shape=[jax.ShapeDtypeStruct((fields, levels, HALO_W), F32)] * 2,
        scratch_shapes=[pltpu.SemaphoreType.DMA((2,))],
        cost_estimate=pl.CostEstimate(flops=0, bytes_accessed=3 * 10**6, transcendentals=0),
    )(even, hbm(state), after)


def gather_halo(pick, index, coef):
    rows = pick(0).shape[0]
    lane = jnp.broadcast_to(jnp.bitwise_and(index, LANES - 1), (rows, LANES))
    part = jnp.broadcast_to(jnp.right_shift(index, 7), (rows, LANES))
    found = jnp.zeros((rows, LANES), F32)
    for h in range(2 * HALO_W // LANES):
        got = jnp.take_along_axis(pick(h), lane, axis=1)
        found = jnp.where(part == h, got, found)
    return found * coef


def rows_of(ref):
    return jnp.concatenate([ref[block : block + 1, :] for block in range(ref.shape[0])], axis=1)


def remap_body(
    one_ref, two_ref, state_ref, ops_ref, local_ref, halo_ref, coef_ref, src_ref, owner_ref, tile_ref, weight_ref,
    star_ref, total_ref, out_ref, window, ops, weights, first_s, second_s, pairs, products, sem,
):
    fields, columns = star_ref.shape
    tiles = columns // LANES
    remaps = weight_ref.shape[0]
    group = out_ref.shape[0] // CHUNK
    parts = 4
    size = remaps // parts
    copies = [
        pltpu.make_async_copy(weight_ref.at[pl.ds(i * size, size)], weights.at[pl.ds(i * size, size)], sem.at[i])
        for i in range(parts)
    ]
    load = pltpu.make_async_copy(state_ref.at[0, :, pl.ds(0, 8), :], window, sem.at[parts])
    load_ops = pltpu.make_async_copy(ops_ref, ops, sem.at[parts + 1])
    load.start()
    load_ops.start()
    for copy in copies:
        copy.start()

    per = HALO_W // LANES

    def pick(h):
        ref = one_ref if h < per else two_ref
        h = h % per
        return ref[:, h * LANES : (h + 1) * LANES]

    blocks = halo_ref.shape[0]
    flow = jnp.concatenate(
        [gather_halo(pick, halo_ref[k : k + 1, :], coef_ref[k : k + 1, :]) for k in range(blocks)], axis=1
    )
    coef = rows_of(coef_ref)
    own = rows_of(local_ref)
    own_tile = jnp.right_shift(own, 7)
    stack = jnp.concatenate([flow, coef], axis=0)
    wide = jnp.concatenate([jnp.where(own_tile == t, stack, 0.0) for t in range(tiles)], axis=0)
    across = jnp.transpose(jnp.bitwise_and(local_ref[...], LANES - 1))
    lane = lax.broadcasted_iota(jnp.int32, (LANES, LANES), 1)
    hot = jnp.concatenate(
        [
            jnp.where(jnp.broadcast_to(across[:, k : k + 1], (LANES, LANES)) == lane, 1.0, 0.0).astype(BF16)
            for k in range(blocks)
        ],
        axis=0,
    )
    spread = sum(mm(part, hot) for part in split3(wide))
    load.wait()
    load_ops.wait()
    for tile in range(tiles):
        where = slice(tile * LANES, (tile + 1) * LANES)
        here = window[:, 0, where]
        mixed = jnp.dot(here, ops[tile], precision=lax.Precision.HIGHEST, preferred_element_type=F32)
        base = tile * (fields + 1)
        total = spread[base + fields : base + fields + 1]
        total_ref[:, where] = jnp.broadcast_to(total, (total_ref.shape[0], LANES))
        star = here + STEP * (mixed + (spread[base : base + fields] - total * here))
        star_ref[:, where] = star
        surface = star.astype(BF16).astype(F32)
        nothing = jnp.zeros_like(surface)
        first_s[tile] = jnp.concatenate([surface, nothing], axis=0)
        second_s[tile] = jnp.concatenate([nothing, surface], axis=0)
    for pair in range(remaps // 2):
        left = first_s[src_ref[2 * pair]]
        right = second_s[src_ref[2 * pair + 1]]
        pairs[pair] = jnp.concatenate([left, right], axis=1)
    for part in range(parts):
        copies[part].wait()
        for pair in range(part * size // 2, (part + 1) * size // 2):
            weight = weights[2 * pair : 2 * pair + 2].reshape(2 * LANES, LANES)
            products[2 * fields * pair : 2 * fields * (pair + 1)] = mm(pairs[pair].astype(BF16), weight)

    owner = owner_ref[...]
    down = lax.broadcasted_iota(jnp.int32, (remaps, remaps), 0)
    right = lax.broadcasted_iota(jnp.int32, (remaps, remaps), 1)
    owner_rows = jnp.broadcast_to(owner, (remaps, remaps))
    owner_columns = jnp.transpose(owner_rows)
    earlier = jnp.where((owner_rows == owner_columns) & (down < right), 1, 0)
    rank = jnp.sum(earlier, axis=0, keepdims=True)
    dest = lax.broadcasted_iota(jnp.int32, (group, remaps), 0)
    named = jnp.broadcast_to(owner, (group, remaps)) == dest
    slots = [named & (jnp.broadcast_to(rank, (group, remaps)) == k) for k in range(2)]
    place = jnp.concatenate([jnp.where(slot, 1.0, 0.0).astype(BF16) for slot in slots], axis=0)
    wanted = tile_ref[...]
    labels = [jnp.max(jnp.where(slot, wanted, -1), axis=1, keepdims=True) for slot in slots]
    side = lax.broadcasted_iota(jnp.int32, (group, LANES), 1)
    note = jnp.where(side == 0, labels[0], jnp.where(side == 1, labels[1], -1))
    out_ref[pl.ds(2 * fields, group, stride=CHUNK), :] = note.astype(F32)
    for field in range(fields):
        value = products[pl.ds(field, remaps, stride=fields), :]
        placed = sum(mm(place, part) for part in split3(value))
        for k in range(2):
            out_ref[pl.ds(k * fields + field, group, stride=CHUNK), :] = placed[k * group : (k + 1) * group]


def remap(one, two, state, ops, edge_local, edge_halo, edge_coef, src, owners, wanted, weight, group):
    _, fields, _, columns = state.shape
    remaps = weight.shape[0]
    blocks = edge_halo.size // LANES
    tiles = columns // LANES
    fold = lambda x: x.reshape(blocks, LANES)
    return pl.pallas_call(
        remap_body,
        in_specs=[vspec()] * 2 + [aspec()] * 2 + [vspec()] * 3 + [sspec(), vspec(), vspec(), aspec()],
        out_specs=[vspec()] * 3,
        out_shape=[
            jax.ShapeDtypeStruct((fields, columns), F32),
            jax.ShapeDtypeStruct((8, columns), F32),
            jax.ShapeDtypeStruct((group * CHUNK, LANES), F32),
        ],
        scratch_shapes=[
            pltpu.VMEM((fields, 8, columns), F32),
            pltpu.VMEM(ops.shape, F32),
            pltpu.VMEM(weight.shape, BF16),
            pltpu.VMEM((tiles, 2 * fields, LANES), F32),
            pltpu.VMEM((tiles, 2 * fields, LANES), F32),
            pltpu.VMEM((remaps // 2, 2 * fields, 2 * LANES), F32),
            pltpu.VMEM((remaps * fields, LANES), F32),
            pltpu.SemaphoreType.DMA((6,)),
        ],
        compiler_params=params(16),
        cost_estimate=pl.CostEstimate(flops=6 * 10**10, bytes_accessed=6 * 10**6, transcendentals=0),
    )(
        one, two, hbm(state), hbm(ops), fold(edge_local), fold(edge_halo), fold(edge_coef), src,
        owners.reshape(1, remaps), wanted.reshape(1, remaps), hbm(weight),
    )


def column_body(
    one_ref, two_ref, local_ref, halo_ref, coef_ref, state_ref, ops_ref, total_ref, star_ref, kappa_ref,
    active_ref, base_ref, gain_ref, flow_hi, flow_lo, work, inv, up, down,
):
    step = pl.program_id(0)
    _, fields, levels, width = state_ref.shape
    rows = fields * levels
    per = HALO_W // LANES
    blocks = halo_ref.shape[0]
    tiles = range(width // LANES)
    cut = [slice(tile * LANES, (tile + 1) * LANES) for tile in tiles]

    @pl.when(step == 0)
    def _():
        def pick(h):
            where = slice((h % per) * LANES, (h % per + 1) * LANES)
            ref = one_ref if h < per else two_ref
            return ref[:, :, where].reshape(rows, LANES)

        for k in range(blocks):
            hi, lo = split2(gather_halo(pick, halo_ref[k : k + 1, :], coef_ref[k : k + 1, :]))
            flow_hi[:, k * LANES : (k + 1) * LANES] = hi
            flow_lo[:, k * LANES : (k + 1) * LANES] = lo

    across = jnp.transpose(local_ref[...] - step * width)
    lane = lax.broadcasted_iota(jnp.int32, (LANES, LANES), 1)
    hot = []
    for k in range(blocks):
        own = jnp.broadcast_to(across[:, k : k + 1], (LANES, LANES)) - lane
        hot.append(jnp.concatenate([jnp.where(own == t * LANES, 1.0, 0.0).astype(BF16) for t in tiles], axis=1))
    hot = jnp.concatenate(hot, axis=0)
    extra = mm(flow_hi[...], hot) + mm(flow_lo[...], hot)
    for tile in tiles:
        here = state_ref[0, :, :, cut[tile]].reshape(rows, LANES)
        a_hi, a_lo = split2(here)
        b_hi, b_lo = split2(ops_ref[tile])
        mixed = mm(a_hi, b_hi) + (mm(a_hi, b_lo) + mm(a_lo, b_hi))
        work[tile] = here + STEP * ((mixed - here * total_ref[0:1, cut[tile]]) + extra[:, cut[tile]])

    depth = lax.broadcasted_iota(jnp.int32, (levels, LANES), 0)
    for tile in tiles:
        count = active_ref[step * len(tiles) + tile]
        down[:, cut[tile]] = jnp.where(depth + 1 < count, -STEP * kappa_ref[0, :, cut[tile]], 0.0)
    last = levels - 1
    upper = down[last : last + 1, :]
    lower = down[last - 1 : last, :]
    inverse = 1.0 / (1.0 - lower - upper)
    ratio = lower * inverse
    inv[last : last + 1, :] = inverse
    up[last : last + 1, :] = upper * inverse
    down[last : last + 1, :] = ratio
    for level in range(last - 1, -1, -1):
        row = slice(level, level + 1)
        upper = lower
        lower = down[level - 1 : level, :] if level else jnp.zeros_like(upper)
        inverse = 1.0 / (1.0 - lower - upper - upper * ratio)
        ratio = lower * inverse
        inv[row, :] = inverse
        up[row, :] = upper * inverse
        down[row, :] = ratio
    gain = RELAX * inverse
    gain_ref[0:1, :] = gain
    for level in range(1, levels):
        gain = -gain * down[level : level + 1, :]
        gain_ref[level : level + 1, :] = gain

    values = [None for _ in tiles]
    for level in range(last, -1, -1):
        row = slice(level, level + 1)
        spot = pl.ds(level, fields, stride=levels)
        for tile in tiles:
            rhs = work[tile, spot, :] if level else RELAX * star_ref[:, cut[tile]]
            scaled = rhs * inv[row, cut[tile]]
            value = values[tile]
            values[tile] = scaled if value is None else scaled - up[row, cut[tile]] * value
            work[tile, spot, :] = values[tile]
    for level in range(1, levels):
        row = slice(level, level + 1)
        spot = pl.ds(level, fields, stride=levels)
        for tile in tiles:
            values[tile] = work[tile, spot, :] - down[row, cut[tile]] * values[tile]
            work[tile, spot, :] = values[tile]
    for tile in tiles:
        base_ref[:, :, cut[tile]] = work[tile].reshape(fields, levels, LANES)


def column_part(one, two, edge_local, edge_halo, edge_coef, state, ops, total, star, kappa, active):
    _, fields, levels, columns = state.shape
    steps = 4
    width = columns // steps
    edges = edge_halo.size
    blocks = edges // LANES
    column = pl.BlockSpec((levels, width), lambda i: (0, i))
    whole = lambda x: pl.BlockSpec(x.shape, lambda i: (0,) * x.ndim)
    lists = [x.reshape(blocks, LANES) for x in (edge_local, edge_halo, edge_coef)]
    return pl.pallas_call(
        column_body,
        grid=(steps,),
        in_specs=[whole(x) for x in (one, two, *lists)]
        + [
            pl.BlockSpec((1, fields, levels, width), lambda i: (0, 0, 0, i)),
            pl.BlockSpec((width // LANES, LANES, LANES), lambda i: (i, 0, 0)),
            pl.BlockSpec((8, width), lambda i: (0, i)),
            pl.BlockSpec((fields, width), lambda i: (0, i)),
            pl.BlockSpec((1, levels, width), lambda i: (0, 0, i)),
            sspec(),
        ],
        out_specs=[pl.BlockSpec((fields, levels, width), lambda i: (0, 0, i)), column],
        out_shape=[
            jax.ShapeDtypeStruct((fields, levels, columns), F32),
            jax.ShapeDtypeStruct((levels, columns), F32),
        ],
        scratch_shapes=[
            pltpu.VMEM((fields * levels, edges), BF16),
            pltpu.VMEM((fields * levels, edges), BF16),
            pltpu.VMEM((width // LANES, fields * levels, LANES), F32),
            pltpu.VMEM((levels, width), F32),
            pltpu.VMEM((levels, width), F32),
            pltpu.VMEM((levels, width), F32),
        ],
        compiler_params=params(24),
        cost_estimate=pl.CostEstimate(flops=6 * 10**10, bytes_accessed=10**7, transcendentals=0),
    )(one, two, *lists, hbm(state), hbm(ops), total, star, hbm(kappa), active)


def gather_body(arrived_ref, _, flux_ref):
    fields, tiles, _ = flux_ref.shape
    sources = arrived_ref.shape[0] // CHUNK
    labels = jnp.transpose(arrived_ref[pl.ds(2 * fields, sources, stride=CHUNK), :])
    tile = lax.broadcasted_iota(jnp.int32, (tiles, sources), 0).astype(F32)
    select = jnp.concatenate(
        [jnp.where(tile == labels[k : k + 1, :], 1.0, 0.0).astype(BF16) for k in range(2)], axis=1
    )
    for field in range(fields):
        value = jnp.concatenate(
            [arrived_ref[pl.ds(k * fields + field, sources, stride=CHUNK), :] for k in range(2)], axis=0
        )
        flux_ref[field] = sum(mm(select, part) for part in split3(value))


def gather_flux(arrived, after, fields, tiles):
    return pl.pallas_call(
        gather_body,
        in_specs=[vspec(), pl.BlockSpec(memory_space=pl.ANY)],
        out_specs=vspec(),
        out_shape=jax.ShapeDtypeStruct((fields, tiles, LANES), F32),
        cost_estimate=pl.CostEstimate(flops=10**6, bytes_accessed=10**6, transcendentals=0),
    )(arrived, after)


def finish_body(base_ref, gain_ref, flux_ref, active_ref, out_ref, flux_out):
    step = pl.program_id(0)
    fields, levels, width = base_ref.shape
    depth = lax.broadcasted_iota(jnp.int32, (levels, LANES), 0)
    for tile in range(width // LANES):
        where = slice(tile * LANES, (tile + 1) * LANES)
        place = step * (width // LANES) + tile
        inside = depth < active_ref[place]
        gain = gain_ref[:, where]
        for field in range(fields):
            flux = flux_ref[field, pl.ds(place, 1), :]
            flux_out[0, field : field + 1, where] = flux
            out_ref[0, field, :, where] = jnp.where(inside, base_ref[field, :, where] + gain * flux, 0.0)


def finish(base, gain, flux, active):
    fields, levels, columns = base.shape
    steps = 4
    width = columns // steps
    return pl.pallas_call(
        finish_body,
        grid=(steps,),
        in_specs=[
            pl.BlockSpec((fields, levels, width), lambda i: (0, 0, i)),
            pl.BlockSpec((levels, width), lambda i: (0, i)),
            pl.BlockSpec(flux.shape, lambda i: (0, 0, 0)),
            sspec(),
        ],
        out_specs=[
            pl.BlockSpec((1, fields, levels, width), lambda i: (0, 0, 0, i)),
            pl.BlockSpec((1, fields, width), lambda i: (0, 0, i)),
        ],
        out_shape=[
            jax.ShapeDtypeStruct((1, fields, levels, columns), F32),
            jax.ShapeDtypeStruct((1, fields, columns), F32),
        ],
        compiler_params=params(24),
        cost_estimate=pl.CostEstimate(flops=10**7, bytes_accessed=6 * 10**6, transcendentals=0),
    )(base, gain, flux, active)


def local(
    state, tile_ops, kappa, active, edge_local, edge_halo, edge_coef, remap_src, remap_owner, remap_tile, remap_weight
):
    _, fields, levels, columns = state.shape
    tiles = tile_ops.shape[1]
    remaps = remap_src.shape[1]
    axes = ("blk", "sub")
    group = lax.axis_size("blk") * lax.axis_size("sub")
    first = [(i, i ^ 1) for i in range(group)]
    second = [(i, (i + 1) % group if i % 2 else (i - 1) % group) for i in range(group)]
    even = (1 - lax.axis_index("sub") % 2).astype(jnp.int32).reshape(1)
    count = active.reshape(tiles)
    halo = jnp.bitwise_xor(edge_halo, HALO_W * even[0])

    top_one, top_two = pack_top(even, state)
    one, two = pack(even, state, top_one)
    top_one = lax.ppermute(top_one, axes, first)
    top_two = lax.ppermute(top_two, axes, second)
    one = lax.ppermute(one, axes, first)
    two = lax.ppermute(two, axes, second)
    star0, total, outgoing = remap(
        top_one, top_two, state, tile_ops[0], edge_local, halo, edge_coef, remap_src.reshape(remaps),
        remap_owner, remap_tile, remap_weight[0], group,
    )
    arrived = lax.all_to_all(
        outgoing.reshape(group, 1, CHUNK * LANES), axes, split_axis=0, concat_axis=0, tiled=True
    )
    base, gain = column_part(
        one, two, edge_local, halo, edge_coef, state, tile_ops[0], total, star0, kappa, count
    )
    flux = gather_flux(arrived.reshape(group * CHUNK, LANES), gain, fields, tiles)
    flux = lax.ppermute(flux, "comp", [(0, 1), (1, 0)])
    return finish(base, gain, flux, count)


def solution(mesh):
    placed = (
        P("comp", None, None, ("blk", "sub")),
        P("comp", ("blk", "sub"), None, None),
        P("comp", None, ("blk", "sub")),
        P("comp", ("blk", "sub")),
        P("comp", ("blk", "sub")),
        P("comp", ("blk", "sub")),
        P("comp", ("blk", "sub")),
        P("comp", ("blk", "sub")),
        P("comp", ("blk", "sub"), None),
        P("comp", ("blk", "sub")),
        P("comp", ("blk", "sub"), None, None),
    )
    return jax.shard_map(
        local,
        mesh=mesh,
        in_specs=placed,
        out_specs=(P("comp", None, None, ("blk", "sub")), P("comp", None, ("blk", "sub"))),
        check_vma=False,
    )
```

```python
import jax
import jax.numpy as jnp
from jax import lax
from jax.experimental import pallas as pl
from jax.experimental.pallas import tpu as pltpu
from jax.sharding import PartitionSpec as P

HALO_W = 512
LANES = 128
STEP = 0.25
RELAX = 0.5
CHUNK = 9
F32 = jnp.float32
BF16 = jnp.bfloat16
VMEM = pltpu.VMEM
SMEM = pltpu.SMEM


def split3(x):
    hi = x.astype(BF16)
    rest = x - hi.astype(F32)
    mid = rest.astype(BF16)
    low = (rest - mid.astype(F32)).astype(BF16)
    return hi, mid, low


def split2(x):
    hi = x.astype(BF16)
    return hi, (x - hi.astype(F32)).astype(BF16)


def mm(a, b):
    return jnp.dot(a, b, preferred_element_type=F32)


def vspec():
    return pl.BlockSpec(memory_space=VMEM)


def sspec():
    return pl.BlockSpec(memory_space=SMEM)


def hbm(x):
    return pltpu.with_memory_space_constraint(x, pltpu.HBM)


def aspec():
    return pl.BlockSpec(memory_space=pltpu.HBM)


def params(mib):
    return pltpu.CompilerParams(vmem_limit_bytes=mib * 1024 * 1024)


def sides(even_ref, columns):
    even = even_ref[0] == 1
    last = columns - HALO_W
    return [pl.multiple_of(jnp.where(even, *pair), LANES) for pair in ((last, 0), (0, last))]


def pack_body(even_ref, state_ref, top_one, top_two, one_ref, two_ref, sem):
    loads = [
        pltpu.make_async_copy(state_ref.at[0, :, :, pl.ds(at, HALO_W)], ref, sem.at[i])
        for i, (at, ref) in enumerate(zip(sides(even_ref, state_ref.shape[3]), (one_ref, two_ref)))
    ]
    for load in loads:
        load.start()
    for load, ref, top in zip(loads, (one_ref, two_ref), (top_one, top_two)):
        load.wait()
        top[...] = ref[:, 0, :]


def pack(even, state):
    _, fields, levels, _ = state.shape
    shape = jax.ShapeDtypeStruct
    return pl.pallas_call(
        pack_body,
        in_specs=[sspec(), aspec()],
        out_specs=[vspec()] * 4,
        out_shape=[shape((fields, HALO_W), F32)] * 2 + [shape((fields, levels, HALO_W), F32)] * 2,
        scratch_shapes=[pltpu.SemaphoreType.DMA((2,))],
        cost_estimate=pl.CostEstimate(flops=6 * 10**10, bytes_accessed=3 * 10**6, transcendentals=0),
    )(even, hbm(state))


def gather_halo(pick, index, coef):
    rows = pick(0).shape[0]
    lane = jnp.broadcast_to(jnp.bitwise_and(index, LANES - 1), (rows, LANES))
    part = jnp.broadcast_to(jnp.right_shift(index, 7), (rows, LANES))
    found = jnp.zeros((rows, LANES), F32)
    for h in range(2 * HALO_W // LANES):
        got = jnp.take_along_axis(pick(h), lane, axis=1)
        found = jnp.where(part == h, got, found)
    return found * coef


def rows_of(ref):
    return jnp.concatenate([ref[block : block + 1, :] for block in range(ref.shape[0])], axis=1)


def remap_body(
    one_ref, two_ref, state_ref, ops_ref, local_ref, halo_ref, coef_ref, src_ref, owner_ref, tile_ref, weight_ref,
    star_ref, total_ref, out_ref, window, weights, first_s, second_s, pairs, products, sem,
):
    fields, columns = star_ref.shape
    tiles = columns // LANES
    remaps = weight_ref.shape[0]
    group = out_ref.shape[0] // CHUNK
    parts = 4
    size = remaps // parts
    copies = [
        pltpu.make_async_copy(weight_ref.at[pl.ds(i * size, size)], weights.at[pl.ds(i * size, size)], sem.at[i])
        for i in range(parts)
    ]
    load = pltpu.make_async_copy(state_ref.at[0, :, pl.ds(0, 8), :], window, sem.at[parts])
    load.start()
    for copy in copies:
        copy.start()

    per = HALO_W // LANES

    def pick(h):
        ref = one_ref if h < per else two_ref
        h = h % per
        return ref[:, h * LANES : (h + 1) * LANES]

    blocks = halo_ref.shape[0]
    flow = jnp.concatenate(
        [gather_halo(pick, halo_ref[k : k + 1, :], coef_ref[k : k + 1, :]) for k in range(blocks)], axis=1
    )
    coef = rows_of(coef_ref)
    own = rows_of(local_ref)
    own_tile = jnp.right_shift(own, 7)
    stack = jnp.concatenate([flow, coef], axis=0)
    wide = jnp.concatenate([jnp.where(own_tile == t, stack, 0.0) for t in range(tiles)], axis=0)
    across = jnp.transpose(jnp.bitwise_and(local_ref[...], LANES - 1))
    lane = lax.broadcasted_iota(jnp.int32, (LANES, LANES), 1)
    hot = jnp.concatenate(
        [
            jnp.where(jnp.broadcast_to(across[:, k : k + 1], (LANES, LANES)) == lane, 1.0, 0.0).astype(BF16)
            for k in range(blocks)
        ],
        axis=0,
    )
    spread = sum(mm(part, hot) for part in split3(wide))
    load.wait()
    for tile in range(tiles):
        where = slice(tile * LANES, (tile + 1) * LANES)
        here = window[:, 0, where]
        mixed = jnp.dot(here, ops_ref[tile], precision=lax.Precision.HIGHEST, preferred_element_type=F32)
        base = tile * (fields + 1)
        total = spread[base + fields : base + fields + 1]
        total_ref[:, where] = jnp.broadcast_to(total, (total_ref.shape[0], LANES))
        star = here + STEP * (mixed + (spread[base : base + fields] - total * here))
        star_ref[:, where] = star
        surface = star.astype(BF16).astype(F32)
        nothing = jnp.zeros_like(surface)
        first_s[tile] = jnp.concatenate([surface, nothing], axis=0)
        second_s[tile] = jnp.concatenate([nothing, surface], axis=0)
    for pair in range(remaps // 2):
        left = first_s[src_ref[2 * pair]]
        right = second_s[src_ref[2 * pair + 1]]
        pairs[pair] = jnp.concatenate([left, right], axis=1)
    for part in range(parts):
        copies[part].wait()
        for pair in range(part * size // 2, (part + 1) * size // 2):
            weight = weights[2 * pair : 2 * pair + 2].reshape(2 * LANES, LANES)
            products[2 * fields * pair : 2 * fields * (pair + 1)] = mm(pairs[pair].astype(BF16), weight)

    owner = owner_ref[...]
    down = lax.broadcasted_iota(jnp.int32, (remaps, remaps), 0)
    right = lax.broadcasted_iota(jnp.int32, (remaps, remaps), 1)
    owner_rows = jnp.broadcast_to(owner, (remaps, remaps))
    owner_columns = jnp.transpose(owner_rows)
    earlier = jnp.where((owner_rows == owner_columns) & (down < right), 1, 0)
    rank = jnp.sum(earlier, axis=0, keepdims=True)
    dest = lax.broadcasted_iota(jnp.int32, (group, remaps), 0)
    named = jnp.broadcast_to(owner, (group, remaps)) == dest
    slots = [named & (jnp.broadcast_to(rank, (group, remaps)) == k) for k in range(2)]
    place = jnp.concatenate([jnp.where(slot, 1.0, 0.0).astype(BF16) for slot in slots], axis=0)
    wanted = tile_ref[...]
    labels = [jnp.max(jnp.where(slot, wanted, -1), axis=1, keepdims=True) for slot in slots]
    side = lax.broadcasted_iota(jnp.int32, (group, LANES), 1)
    note = jnp.where(side == 0, labels[0], jnp.where(side == 1, labels[1], -1))
    out_ref[pl.ds(2 * fields, group, stride=CHUNK), :] = note.astype(F32)
    for field in range(fields):
        value = products[pl.ds(field, remaps, stride=fields), :]
        placed = sum(mm(place, part) for part in split3(value))
        for k in range(2):
            out_ref[pl.ds(k * fields + field, group, stride=CHUNK), :] = placed[k * group : (k + 1) * group]


def remap(one, two, state, ops, edge_local, edge_halo, edge_coef, src, owners, wanted, weight, group):
    _, fields, _, columns = state.shape
    remaps = weight.shape[0]
    blocks = edge_halo.size // LANES
    tiles = columns // LANES
    fold = lambda x: x.reshape(blocks, LANES)
    return pl.pallas_call(
        remap_body,
        in_specs=[vspec()] * 2 + [aspec()] + [vspec()] * 4 + [sspec(), vspec(), vspec(), aspec()],
        out_specs=[vspec()] * 3,
        out_shape=[
            jax.ShapeDtypeStruct((fields, columns), F32),
            jax.ShapeDtypeStruct((8, columns), F32),
            jax.ShapeDtypeStruct((group * CHUNK, LANES), F32),
        ],
        scratch_shapes=[
            pltpu.VMEM((fields, 8, columns), F32),
            pltpu.VMEM(weight.shape, BF16),
            pltpu.VMEM((tiles, 2 * fields, LANES), F32),
            pltpu.VMEM((tiles, 2 * fields, LANES), F32),
            pltpu.VMEM((remaps // 2, 2 * fields, 2 * LANES), F32),
            pltpu.VMEM((remaps * fields, LANES), F32),
            pltpu.SemaphoreType.DMA((5,)),
        ],
        compiler_params=params(16),
        cost_estimate=pl.CostEstimate(flops=6 * 10**10, bytes_accessed=6 * 10**6, transcendentals=0),
    )(
        one, two, hbm(state), ops, fold(edge_local), fold(edge_halo), fold(edge_coef), src,
        owners.reshape(1, remaps), wanted.reshape(1, remaps), hbm(weight),
    )


def column_body(
    one_ref, two_ref, local_ref, halo_ref, coef_ref, state_ref, ops_ref, total_ref, star_ref, kappa_ref,
    active_ref, base_ref, gain_ref, token_ref, flow_hi, flow_lo, work, inv, up, down,
):
    step = pl.program_id(0)
    token_ref[...] = jnp.zeros_like(token_ref)
    _, fields, levels, width = state_ref.shape
    rows = fields * levels
    per = HALO_W // LANES
    blocks = halo_ref.shape[0]
    tiles = range(width // LANES)
    cut = [slice(tile * LANES, (tile + 1) * LANES) for tile in tiles]

    @pl.when(step == 0)
    def _():
        def pick(h):
            where = slice((h % per) * LANES, (h % per + 1) * LANES)
            ref = one_ref if h < per else two_ref
            return ref[:, :, where].reshape(rows, LANES)

        down_h = lax.broadcasted_iota(jnp.int32, (2 * HALO_W, LANES), 0)
        parts = split2(jnp.concatenate([pick(h) for h in range(2 * per)], axis=1))
        for k in range(0, blocks, 2):
            rows_k = [slice(k + j, k + j + 1) for j in range(2)]
            here = [jnp.where(down_h == halo_ref[row, :], 1.0, 0.0).astype(BF16) for row in rows_k]
            here = jnp.concatenate(here, axis=1)
            coef = jnp.concatenate([coef_ref[row, :] for row in rows_k], axis=1)
            hi, lo = split2((mm(parts[0], here) + mm(parts[1], here)) * coef)
            flow_hi[:, k * LANES : (k + 2) * LANES] = hi
            flow_lo[:, k * LANES : (k + 2) * LANES] = lo

    across = jnp.transpose(local_ref[...] - step * width)
    lane = lax.broadcasted_iota(jnp.int32, (LANES, LANES), 1)
    hot = []
    for k in range(blocks):
        own = jnp.broadcast_to(across[:, k : k + 1], (LANES, LANES)) - lane
        hot.append(jnp.concatenate([jnp.where(own == t * LANES, 1.0, 0.0).astype(BF16) for t in tiles], axis=1))
    hot = jnp.concatenate(hot, axis=0)
    extra = mm(flow_hi[...], hot) + mm(flow_lo[...], hot)
    for tile in tiles:
        here = state_ref[0, :, :, cut[tile]].reshape(rows, LANES)
        both = jnp.concatenate(split2(ops_ref[tile]), axis=1)
        mixed = mm(jnp.concatenate(split2(here), axis=1), jnp.concatenate([both, both], axis=0))
        mixed = mixed[:, :LANES] + mixed[:, LANES:]
        work[tile] = here + STEP * ((mixed - here * total_ref[0:1, cut[tile]]) + extra[:, cut[tile]])

    depth = lax.broadcasted_iota(jnp.int32, (levels, LANES), 0)
    for tile in tiles:
        count = active_ref[step * len(tiles) + tile]
        down[:, cut[tile]] = jnp.where(depth + 1 < count, -STEP * kappa_ref[0, :, cut[tile]], 0.0)
    last = levels - 1
    upper = down[last : last + 1, :]
    lower = down[last - 1 : last, :]
    inverse = 1.0 / (1.0 - lower - upper)
    ratio = lower * inverse
    inv[last : last + 1, :] = inverse
    up[last : last + 1, :] = upper * inverse
    down[last : last + 1, :] = ratio
    for level in range(last - 1, -1, -1):
        row = slice(level, level + 1)
        upper = lower
        lower = down[level - 1 : level, :] if level else jnp.zeros_like(upper)
        inverse = 1.0 / (1.0 - lower - upper - upper * ratio)
        ratio = lower * inverse
        inv[row, :] = inverse
        up[row, :] = upper * inverse
        down[row, :] = ratio
    gain = RELAX * inverse
    gain_ref[0:1, :] = gain
    for level in range(1, levels):
        gain = -gain * down[level : level + 1, :]
        gain_ref[level : level + 1, :] = gain

    values = [None for _ in tiles]
    for level in range(last, -1, -1):
        row = slice(level, level + 1)
        spot = pl.ds(level, fields, stride=levels)
        for tile in tiles:
            rhs = work[tile, spot, :] if level else RELAX * star_ref[:, cut[tile]]
            scaled = rhs * inv[row, cut[tile]]
            value = values[tile]
            values[tile] = scaled if value is None else scaled - up[row, cut[tile]] * value
            work[tile, spot, :] = values[tile]
    for level in range(1, levels):
        row = slice(level, level + 1)
        spot = pl.ds(level, fields, stride=levels)
        for tile in tiles:
            values[tile] = work[tile, spot, :] - down[row, cut[tile]] * values[tile]
            work[tile, spot, :] = values[tile]
    for tile in tiles:
        base_ref[:, :, cut[tile]] = work[tile].reshape(fields, levels, LANES)


def column_part(one, two, edge_local, edge_halo, edge_coef, state, ops, total, star, kappa, active):
    _, fields, levels, columns = state.shape
    steps = 4
    width = columns // steps
    edges = edge_halo.size
    blocks = edges // LANES
    column = pl.BlockSpec((levels, width), lambda i: (0, i))
    whole = lambda x: pl.BlockSpec(x.shape, lambda i: (0,) * x.ndim)
    lists = [x.reshape(blocks, LANES) for x in (edge_local, edge_halo, edge_coef)]
    return pl.pallas_call(
        column_body,
        grid=(steps,),
        in_specs=[whole(x) for x in (one, two, *lists)]
        + [
            pl.BlockSpec((1, fields, levels, width), lambda i: (0, 0, 0, i)),
            pl.BlockSpec((width // LANES, LANES, LANES), lambda i: (i, 0, 0)),
            pl.BlockSpec((8, width), lambda i: (0, i)),
            pl.BlockSpec((fields, width), lambda i: (0, i)),
            pl.BlockSpec((1, levels, width), lambda i: (0, 0, i)),
            sspec(),
        ],
        out_specs=[
            pl.BlockSpec((fields, levels, width), lambda i: (0, 0, i)),
            column,
            pl.BlockSpec((8, LANES), lambda i: (0, 0)),
        ],
        out_shape=[
            jax.ShapeDtypeStruct((fields, levels, columns), F32),
            jax.ShapeDtypeStruct((levels, columns), F32),
            jax.ShapeDtypeStruct((8, LANES), F32),
        ],
        scratch_shapes=[
            pltpu.VMEM((fields * levels, edges), BF16),
            pltpu.VMEM((fields * levels, edges), BF16),
            pltpu.VMEM((width // LANES, fields * levels, LANES), F32),
            pltpu.VMEM((levels, width), F32),
            pltpu.VMEM((levels, width), F32),
            pltpu.VMEM((levels, width), F32),
        ],
        compiler_params=params(24),
        cost_estimate=pl.CostEstimate(flops=6 * 10**10, bytes_accessed=10**7, transcendentals=0),
    )(hbm(one), hbm(two), *lists, hbm(state), hbm(ops), total, star, hbm(kappa), active)


def gather_body(arrived_ref, _, flux_ref):
    fields, tiles, _ = flux_ref.shape
    sources = arrived_ref.shape[0] // CHUNK
    labels = jnp.transpose(arrived_ref[pl.ds(2 * fields, sources, stride=CHUNK), :])
    tile = lax.broadcasted_iota(jnp.int32, (tiles, sources), 0).astype(F32)
    select = jnp.concatenate(
        [jnp.where(tile == labels[k : k + 1, :], 1.0, 0.0).astype(BF16) for k in range(2)], axis=1
    )
    for field in range(fields):
        value = jnp.concatenate(
            [arrived_ref[pl.ds(k * fields + field, sources, stride=CHUNK), :] for k in range(2)], axis=0
        )
        flux_ref[field] = sum(mm(select, part) for part in split3(value))


def gather_flux(arrived, after, fields, tiles):
    return pl.pallas_call(
        gather_body,
        in_specs=[vspec(), pl.BlockSpec(memory_space=pl.ANY)],
        out_specs=vspec(),
        out_shape=jax.ShapeDtypeStruct((fields, tiles, LANES), F32),
        cost_estimate=pl.CostEstimate(flops=10**6, bytes_accessed=10**6, transcendentals=0),
    )(hbm(arrived), after)


def finish_body(base_ref, gain_ref, flux_ref, active_ref, out_ref, flux_out, result, sem):
    fields, levels, columns = base_ref.shape
    steps = result.shape[0]
    width = columns // steps
    stores = [
        pltpu.make_async_copy(result.at[i], out_ref.at[0, :, :, pl.ds(i * width, width)], sem.at[i])
        for i in range(steps)
    ]
    depth = lax.broadcasted_iota(jnp.int32, (levels, LANES), 0)
    for i in range(steps):
        for tile in range(width // LANES):
            place = i * (width // LANES) + tile
            whole = slice(place * LANES, (place + 1) * LANES)
            where = slice(tile * LANES, (tile + 1) * LANES)
            inside = depth < active_ref[place]
            gain = gain_ref[:, whole]
            for field in range(fields):
                flux = flux_ref[field, place : place + 1, :]
                flux_out[0, field : field + 1, whole] = flux
                result[i, field, :, where] = jnp.where(inside, base_ref[field, :, whole] + gain * flux, 0.0)
        stores[i].start()
    for store in stores:
        store.wait()


def finish(base, gain, flux, active):
    fields, levels, columns = base.shape
    steps = 4
    return pl.pallas_call(
        finish_body,
        in_specs=[vspec(), vspec(), vspec(), sspec()],
        out_specs=[aspec(), vspec()],
        out_shape=[
            jax.ShapeDtypeStruct((1, fields, levels, columns), F32),
            jax.ShapeDtypeStruct((1, fields, columns), F32),
        ],
        scratch_shapes=[
            pltpu.VMEM((steps, fields, levels, columns // steps), F32),
            pltpu.SemaphoreType.DMA((steps,)),
        ],
        compiler_params=params(16),
        cost_estimate=pl.CostEstimate(flops=10**7, bytes_accessed=6 * 10**6, transcendentals=0),
    )(base, gain, flux, active)


def local(
    state, tile_ops, kappa, active, edge_local, edge_halo, edge_coef, remap_src, remap_owner, remap_tile, remap_weight
):
    _, fields, levels, columns = state.shape
    tiles = tile_ops.shape[1]
    remaps = remap_src.shape[1]
    axes = ("blk", "sub")
    group = lax.axis_size("blk") * lax.axis_size("sub")
    first = [(i, i ^ 1) for i in range(group)]
    second = [(i, (i + 1) % group if i % 2 else (i - 1) % group) for i in range(group)]
    even = (1 - lax.axis_index("sub") % 2).astype(jnp.int32).reshape(1)
    count = active.reshape(tiles)
    halo = jnp.bitwise_xor(edge_halo, HALO_W * even[0])

    top_one, top_two, one, two = pack(even, state)
    top_one = lax.ppermute(top_one, axes, first)
    top_two = lax.ppermute(top_two, axes, second)
    one = lax.ppermute(one, axes, first)
    two = lax.ppermute(two, axes, second)
    star0, total, outgoing = remap(
        top_one, top_two, state, tile_ops[0], edge_local, halo, edge_coef, remap_src.reshape(remaps),
        remap_owner, remap_tile, remap_weight[0], group,
    )
    arrived = lax.all_to_all(
        outgoing.reshape(group, 1, CHUNK * LANES), axes, split_axis=0, concat_axis=0, tiled=True
    )
    base, gain, token = column_part(
        one, two, edge_local, halo, edge_coef, state, tile_ops[0], total, star0, kappa, count
    )
    flux = gather_flux(arrived.reshape(group * CHUNK, LANES), token, fields, tiles)
    flux = lax.ppermute(flux, "comp", [(0, 1), (1, 0)])
    return finish(base, gain, flux, count)


def solution(mesh):
    placed = (
        P("comp", None, None, ("blk", "sub")),
        P("comp", ("blk", "sub"), None, None),
        P("comp", None, ("blk", "sub")),
        P("comp", ("blk", "sub")),
        P("comp", ("blk", "sub")),
        P("comp", ("blk", "sub")),
        P("comp", ("blk", "sub")),
        P("comp", ("blk", "sub")),
        P("comp", ("blk", "sub"), None),
        P("comp", ("blk", "sub")),
        P("comp", ("blk", "sub"), None, None),
    )
    return jax.shard_map(
        local,
        mesh=mesh,
        in_specs=placed,
        out_specs=(P("comp", None, None, ("blk", "sub")), P("comp", None, ("blk", "sub"))),
        check_vma=False,
    )
```

```python
import jax
import jax.numpy as jnp
from jax import lax
from jax.experimental import pallas as pl
from jax.experimental.pallas import tpu as pltpu
from jax.sharding import PartitionSpec as P

HALO_W = 512
LANES = 128
STEP = 0.25
RELAX = 0.5
CHUNK = 9
F32 = jnp.float32
BF16 = jnp.bfloat16
VMEM = pltpu.VMEM
SMEM = pltpu.SMEM


def split3(x):
    hi = x.astype(BF16)
    rest = x - hi.astype(F32)
    mid = rest.astype(BF16)
    low = (rest - mid.astype(F32)).astype(BF16)
    return hi, mid, low


def split2(x):
    hi = x.astype(BF16)
    return hi, (x - hi.astype(F32)).astype(BF16)


def mm(a, b):
    return jnp.dot(a, b, preferred_element_type=F32)


def vspec():
    return pl.BlockSpec(memory_space=VMEM)


def sspec():
    return pl.BlockSpec(memory_space=SMEM)


def hbm(x):
    return pltpu.with_memory_space_constraint(x, pltpu.HBM)


def aspec():
    return pl.BlockSpec(memory_space=pltpu.HBM)


def params(mib):
    return pltpu.CompilerParams(vmem_limit_bytes=mib * 1024 * 1024)


def sides(even_ref, columns):
    even = even_ref[0] == 1
    last = columns - HALO_W
    return [pl.multiple_of(jnp.where(even, *pair), LANES) for pair in ((last, 0), (0, last))]


def pack_body(even_ref, state_ref, top_one, top_two, one_ref, two_ref, sem):
    loads = [
        pltpu.make_async_copy(state_ref.at[0, :, :, pl.ds(at, HALO_W)], ref, sem.at[i])
        for i, (at, ref) in enumerate(zip(sides(even_ref, state_ref.shape[3]), (one_ref, two_ref)))
    ]
    for load in loads:
        load.start()
    for load, ref, top in zip(loads, (one_ref, two_ref), (top_one, top_two)):
        load.wait()
        top[...] = ref[:, 0, :]


def pack(even, state):
    _, fields, levels, _ = state.shape
    shape = jax.ShapeDtypeStruct
    return pl.pallas_call(
        pack_body,
        in_specs=[sspec(), aspec()],
        out_specs=[vspec()] * 4,
        out_shape=[shape((fields, HALO_W), F32)] * 2 + [shape((fields, levels, HALO_W), F32)] * 2,
        scratch_shapes=[pltpu.SemaphoreType.DMA((2,))],
        cost_estimate=pl.CostEstimate(flops=6 * 10**10, bytes_accessed=3 * 10**6, transcendentals=0),
    )(even, hbm(state))


def gather_halo(pick, index, coef):
    rows = pick(0).shape[0]
    lane = jnp.broadcast_to(jnp.bitwise_and(index, LANES - 1), (rows, LANES))
    part = jnp.broadcast_to(jnp.right_shift(index, 7), (rows, LANES))
    found = jnp.zeros((rows, LANES), F32)
    for h in range(2 * HALO_W // LANES):
        got = jnp.take_along_axis(pick(h), lane, axis=1)
        found = jnp.where(part == h, got, found)
    return found * coef


def rows_of(ref):
    return jnp.concatenate([ref[block : block + 1, :] for block in range(ref.shape[0])], axis=1)


def remap_body(
    one_ref, two_ref, state_ref, ops_ref, local_ref, halo_ref, coef_ref, src_ref, owner_ref, tile_ref, weight_ref,
    star_ref, total_ref, out_ref, window, weights, first_s, second_s, pairs, products, sem,
):
    fields, columns = star_ref.shape
    tiles = columns // LANES
    remaps = weight_ref.shape[0]
    group = out_ref.shape[0] // CHUNK
    parts = 4
    size = remaps // parts
    copies = [
        pltpu.make_async_copy(weight_ref.at[pl.ds(i * size, size)], weights.at[pl.ds(i * size, size)], sem.at[i])
        for i in range(parts)
    ]
    load = pltpu.make_async_copy(state_ref.at[0, :, pl.ds(0, 8), :], window, sem.at[parts])
    load.start()
    for copy in copies:
        copy.start()

    per = HALO_W // LANES

    def pick(h):
        ref = one_ref if h < per else two_ref
        h = h % per
        return ref[:, h * LANES : (h + 1) * LANES]

    blocks = halo_ref.shape[0]
    flow = jnp.concatenate(
        [gather_halo(pick, halo_ref[k : k + 1, :], coef_ref[k : k + 1, :]) for k in range(blocks)], axis=1
    )
    coef = rows_of(coef_ref)
    own = rows_of(local_ref)
    own_tile = jnp.right_shift(own, 7)
    stack = jnp.concatenate([flow, coef], axis=0)
    wide = jnp.concatenate([jnp.where(own_tile == t, stack, 0.0) for t in range(tiles)], axis=0)
    across = jnp.transpose(jnp.bitwise_and(local_ref[...], LANES - 1))
    lane = lax.broadcasted_iota(jnp.int32, (LANES, LANES), 1)
    hot = jnp.concatenate(
        [
            jnp.where(jnp.broadcast_to(across[:, k : k + 1], (LANES, LANES)) == lane, 1.0, 0.0).astype(BF16)
            for k in range(blocks)
        ],
        axis=0,
    )
    spread = sum(mm(part, hot) for part in split3(wide))
    load.wait()
    for tile in range(tiles):
        where = slice(tile * LANES, (tile + 1) * LANES)
        here = window[:, 0, where]
        mixed = jnp.dot(here, ops_ref[tile], precision=lax.Precision.HIGHEST, preferred_element_type=F32)
        base = tile * (fields + 1)
        total = spread[base + fields : base + fields + 1]
        total_ref[:, where] = jnp.broadcast_to(total, (total_ref.shape[0], LANES))
        star = here + STEP * (mixed + (spread[base : base + fields] - total * here))
        star_ref[:, where] = star
        surface = star.astype(BF16).astype(F32)
        nothing = jnp.zeros_like(surface)
        first_s[tile] = jnp.concatenate([surface, nothing], axis=0)
        second_s[tile] = jnp.concatenate([nothing, surface], axis=0)
    for pair in range(remaps // 2):
        left = first_s[src_ref[2 * pair]]
        right = second_s[src_ref[2 * pair + 1]]
        pairs[pair] = jnp.concatenate([left, right], axis=1)
    for part in range(parts):
        copies[part].wait()
        for pair in range(part * size // 2, (part + 1) * size // 2):
            weight = weights[2 * pair : 2 * pair + 2].reshape(2 * LANES, LANES)
            products[2 * fields * pair : 2 * fields * (pair + 1)] = mm(pairs[pair].astype(BF16), weight)

    owner = owner_ref[...]
    down = lax.broadcasted_iota(jnp.int32, (remaps, remaps), 0)
    right = lax.broadcasted_iota(jnp.int32, (remaps, remaps), 1)
    owner_rows = jnp.broadcast_to(owner, (remaps, remaps))
    owner_columns = jnp.transpose(owner_rows)
    earlier = jnp.where((owner_rows == owner_columns) & (down < right), 1, 0)
    rank = jnp.sum(earlier, axis=0, keepdims=True)
    dest = lax.broadcasted_iota(jnp.int32, (group, remaps), 0)
    named = jnp.broadcast_to(owner, (group, remaps)) == dest
    slots = [named & (jnp.broadcast_to(rank, (group, remaps)) == k) for k in range(2)]
    place = jnp.concatenate([jnp.where(slot, 1.0, 0.0).astype(BF16) for slot in slots], axis=0)
    wanted = tile_ref[...]
    labels = [jnp.max(jnp.where(slot, wanted, -1), axis=1, keepdims=True) for slot in slots]
    side = lax.broadcasted_iota(jnp.int32, (group, LANES), 1)
    note = jnp.where(side == 0, labels[0], jnp.where(side == 1, labels[1], -1))
    out_ref[pl.ds(2 * fields, group, stride=CHUNK), :] = note.astype(F32)
    for field in range(fields):
        value = products[pl.ds(field, remaps, stride=fields), :]
        placed = sum(mm(place, part) for part in split3(value))
        for k in range(2):
            out_ref[pl.ds(k * fields + field, group, stride=CHUNK), :] = placed[k * group : (k + 1) * group]


def remap(one, two, state, ops, edge_local, edge_halo, edge_coef, src, owners, wanted, weight, group):
    _, fields, _, columns = state.shape
    remaps = weight.shape[0]
    blocks = edge_halo.size // LANES
    tiles = columns // LANES
    fold = lambda x: x.reshape(blocks, LANES)
    return pl.pallas_call(
        remap_body,
        in_specs=[vspec()] * 2 + [aspec()] + [vspec()] * 4 + [sspec(), vspec(), vspec(), aspec()],
        out_specs=[vspec()] * 3,
        out_shape=[
            jax.ShapeDtypeStruct((fields, columns), F32),
            jax.ShapeDtypeStruct((8, columns), F32),
            jax.ShapeDtypeStruct((group * CHUNK, LANES), F32),
        ],
        scratch_shapes=[
            pltpu.VMEM((fields, 8, columns), F32),
            pltpu.VMEM(weight.shape, BF16),
            pltpu.VMEM((tiles, 2 * fields, LANES), F32),
            pltpu.VMEM((tiles, 2 * fields, LANES), F32),
            pltpu.VMEM((remaps // 2, 2 * fields, 2 * LANES), F32),
            pltpu.VMEM((remaps * fields, LANES), F32),
            pltpu.SemaphoreType.DMA((5,)),
        ],
        compiler_params=params(16),
        cost_estimate=pl.CostEstimate(flops=6 * 10**10, bytes_accessed=6 * 10**6, transcendentals=0),
    )(
        one, two, hbm(state), ops, fold(edge_local), fold(edge_halo), fold(edge_coef), src,
        owners.reshape(1, remaps), wanted.reshape(1, remaps), hbm(weight),
    )


def column_body(
    one_ref, two_ref, local_ref, halo_ref, coef_ref, state_ref, ops_ref, total_ref, star_ref, kappa_ref,
    active_ref, base_ref, gain_ref, token_ref, flow_hi, flow_lo, work, inv, up, down,
):
    step = pl.program_id(0)
    token_ref[...] = jnp.zeros_like(token_ref)
    _, fields, levels, width = state_ref.shape
    rows = fields * levels
    per = HALO_W // LANES
    blocks = halo_ref.shape[0]
    tiles = range(width // LANES)
    cut = [slice(tile * LANES, (tile + 1) * LANES) for tile in tiles]

    @pl.when(step == 0)
    def _():
        def pick(h):
            where = slice((h % per) * LANES, (h % per + 1) * LANES)
            ref = one_ref if h < per else two_ref
            return ref[:, :, where].reshape(rows, LANES)

        down_h = lax.broadcasted_iota(jnp.int32, (2 * HALO_W, LANES), 0)
        parts = split2(jnp.concatenate([pick(h) for h in range(2 * per)], axis=1))
        for k in range(0, blocks, 2):
            rows_k = [slice(k + j, k + j + 1) for j in range(2)]
            here = [jnp.where(down_h == halo_ref[row, :], 1.0, 0.0).astype(BF16) for row in rows_k]
            here = jnp.concatenate(here, axis=1)
            coef = jnp.concatenate([coef_ref[row, :] for row in rows_k], axis=1)
            hi, lo = split2((mm(parts[0], here) + mm(parts[1], here)) * coef)
            flow_hi[:, k * LANES : (k + 2) * LANES] = hi
            flow_lo[:, k * LANES : (k + 2) * LANES] = lo

    across = jnp.transpose(local_ref[...] - step * width)
    lane = lax.broadcasted_iota(jnp.int32, (LANES, LANES), 1)
    hot = []
    for k in range(blocks):
        own = jnp.broadcast_to(across[:, k : k + 1], (LANES, LANES)) - lane
        hot.append(jnp.concatenate([jnp.where(own == t * LANES, 1.0, 0.0).astype(BF16) for t in tiles], axis=1))
    hot = jnp.concatenate(hot, axis=0)
    extra = mm(flow_hi[...], hot) + mm(flow_lo[...], hot)
    for tile in tiles:
        here = state_ref[0, :, :, cut[tile]].reshape(rows, LANES)
        both = jnp.concatenate(split2(ops_ref[tile]), axis=1)
        mixed = mm(jnp.concatenate(split2(here), axis=1), jnp.concatenate([both, both], axis=0))
        mixed = mixed[:, :LANES] + mixed[:, LANES:]
        work[tile] = here + STEP * ((mixed - here * total_ref[0:1, cut[tile]]) + extra[:, cut[tile]])

    depth = lax.broadcasted_iota(jnp.int32, (levels, LANES), 0)
    for tile in tiles:
        count = active_ref[step * len(tiles) + tile]
        down[:, cut[tile]] = jnp.where(depth + 1 < count, -STEP * kappa_ref[0, :, cut[tile]], 0.0)
    last = levels - 1
    upper = down[last : last + 1, :]
    lower = down[last - 1 : last, :]
    inverse = 1.0 / (1.0 - lower - upper)
    ratio = lower * inverse
    inv[last : last + 1, :] = inverse
    up[last : last + 1, :] = upper * inverse
    down[last : last + 1, :] = ratio
    for level in range(last - 1, -1, -1):
        row = slice(level, level + 1)
        upper = lower
        lower = down[level - 1 : level, :] if level else jnp.zeros_like(upper)
        inverse = 1.0 / (1.0 - lower - upper - upper * ratio)
        ratio = lower * inverse
        inv[row, :] = inverse
        up[row, :] = upper * inverse
        down[row, :] = ratio
    gain = RELAX * inverse
    gain_ref[0:1, :] = gain
    for level in range(1, levels):
        gain = -gain * down[level : level + 1, :]
        gain_ref[level : level + 1, :] = gain

    values = [None for _ in tiles]
    for level in range(last, -1, -1):
        row = slice(level, level + 1)
        spot = pl.ds(level, fields, stride=levels)
        for tile in tiles:
            rhs = work[tile, spot, :] if level else RELAX * star_ref[:, cut[tile]]
            scaled = rhs * inv[row, cut[tile]]
            value = values[tile]
            values[tile] = scaled if value is None else scaled - up[row, cut[tile]] * value
            work[tile, spot, :] = values[tile]
    for level in range(1, levels):
        row = slice(level, level + 1)
        spot = pl.ds(level, fields, stride=levels)
        for tile in tiles:
            values[tile] = work[tile, spot, :] - down[row, cut[tile]] * values[tile]
            work[tile, spot, :] = values[tile]
    for tile in tiles:
        base_ref[:, :, cut[tile]] = work[tile].reshape(fields, levels, LANES)


def column_part(one, two, edge_local, edge_halo, edge_coef, state, ops, total, star, kappa, active):
    _, fields, levels, columns = state.shape
    steps = 4
    width = columns // steps
    edges = edge_halo.size
    blocks = edges // LANES
    column = pl.BlockSpec((levels, width), lambda i: (0, i))
    whole = lambda x: pl.BlockSpec(x.shape, lambda i: (0,) * x.ndim)
    lists = [x.reshape(blocks, LANES) for x in (edge_local, edge_halo, edge_coef)]
    return pl.pallas_call(
        column_body,
        grid=(steps,),
        in_specs=[whole(x) for x in (one, two, *lists)]
        + [
            pl.BlockSpec((1, fields, levels, width), lambda i: (0, 0, 0, i)),
            pl.BlockSpec((width // LANES, LANES, LANES), lambda i: (i, 0, 0)),
            pl.BlockSpec((8, width), lambda i: (0, i)),
            pl.BlockSpec((fields, width), lambda i: (0, i)),
            pl.BlockSpec((1, levels, width), lambda i: (0, 0, i)),
            sspec(),
        ],
        out_specs=[
            pl.BlockSpec((fields, levels, width), lambda i: (0, 0, i)),
            column,
            pl.BlockSpec((8, LANES), lambda i: (0, 0)),
        ],
        out_shape=[
            jax.ShapeDtypeStruct((fields, levels, columns), F32),
            jax.ShapeDtypeStruct((levels, columns), F32),
            pltpu.HBM((8, LANES), F32),
        ],
        scratch_shapes=[
            pltpu.VMEM((fields * levels, edges), BF16),
            pltpu.VMEM((fields * levels, edges), BF16),
            pltpu.VMEM((width // LANES, fields * levels, LANES), F32),
            pltpu.VMEM((levels, width), F32),
            pltpu.VMEM((levels, width), F32),
            pltpu.VMEM((levels, width), F32),
        ],
        compiler_params=params(24),
        cost_estimate=pl.CostEstimate(flops=6 * 10**10, bytes_accessed=10**7, transcendentals=0),
    )(hbm(one), hbm(two), *lists, hbm(state), hbm(ops), total, star, hbm(kappa), active)


def finish_body(base_ref, gain_ref, arrived_ref, active_ref, out_ref, flux_out, flux_ref, result, sem):
    fields, levels, columns = base_ref.shape
    steps = result.shape[0]
    width = columns // steps
    stores = [
        pltpu.make_async_copy(result.at[i], out_ref.at[0, :, :, pl.ds(i * width, width)], sem.at[i])
        for i in range(steps)
    ]
    tiles = columns // LANES
    sources = arrived_ref.shape[0] // CHUNK
    labels = jnp.transpose(arrived_ref[pl.ds(2 * fields, sources, stride=CHUNK), :])
    named = lax.broadcasted_iota(jnp.int32, (tiles, sources), 0).astype(F32)
    select = jnp.concatenate(
        [jnp.where(named == labels[k : k + 1, :], 1.0, 0.0).astype(BF16) for k in range(2)], axis=1
    )
    for field in range(fields):
        value = jnp.concatenate(
            [arrived_ref[pl.ds(k * fields + field, sources, stride=CHUNK), :] for k in range(2)], axis=0
        )
        flux_ref[field] = sum(mm(select, part) for part in split3(value))
    depth = lax.broadcasted_iota(jnp.int32, (levels, LANES), 0)
    for i in range(steps):
        for tile in range(width // LANES):
            place = i * (width // LANES) + tile
            whole = slice(place * LANES, (place + 1) * LANES)
            where = slice(tile * LANES, (tile + 1) * LANES)
            inside = depth < active_ref[place]
            gain = gain_ref[:, whole]
            for field in range(fields):
                flux = flux_ref[field, place : place + 1, :]
                flux_out[0, field : field + 1, whole] = flux
                result[i, field, :, where] = jnp.where(inside, base_ref[field, :, whole] + gain * flux, 0.0)
        stores[i].start()
    for store in stores:
        store.wait()


def finish(base, gain, arrived, active):
    fields, levels, columns = base.shape
    steps = 4
    return pl.pallas_call(
        finish_body,
        in_specs=[vspec(), vspec(), vspec(), sspec()],
        out_specs=[aspec(), vspec()],
        out_shape=[
            jax.ShapeDtypeStruct((1, fields, levels, columns), F32),
            jax.ShapeDtypeStruct((1, fields, columns), F32),
        ],
        scratch_shapes=[
            pltpu.VMEM((fields, columns // LANES, LANES), F32),
            pltpu.VMEM((steps, fields, levels, columns // steps), F32),
            pltpu.SemaphoreType.DMA((steps,)),
        ],
        compiler_params=params(16),
        cost_estimate=pl.CostEstimate(flops=10**7, bytes_accessed=6 * 10**6, transcendentals=0),
    )(base, gain, arrived, active)


def after_body(value_ref, token_ref, out_ref):
    pass


def after(value, token):
    anywhere = pl.BlockSpec(memory_space=pl.ANY)
    return pl.pallas_call(
        after_body,
        in_specs=[anywhere, anywhere],
        out_specs=anywhere,
        out_shape=jax.ShapeDtypeStruct(value.shape, value.dtype),
        input_output_aliases={0: 0},
        cost_estimate=pl.CostEstimate(flops=0, bytes_accessed=0, transcendentals=0),
    )(value, token)


def local(
    state, tile_ops, kappa, active, edge_local, edge_halo, edge_coef, remap_src, remap_owner, remap_tile, remap_weight
):
    _, fields, levels, columns = state.shape
    tiles = tile_ops.shape[1]
    remaps = remap_src.shape[1]
    axes = ("blk", "sub")
    group = lax.axis_size("blk") * lax.axis_size("sub")
    first = [(i, i ^ 1) for i in range(group)]
    second = [(i, (i + 1) % group if i % 2 else (i - 1) % group) for i in range(group)]
    even = (1 - lax.axis_index("sub") % 2).astype(jnp.int32).reshape(1)
    count = active.reshape(tiles)
    halo = jnp.bitwise_xor(edge_halo, HALO_W * even[0])

    top_one, top_two, one, two = pack(even, state)
    top_one = lax.ppermute(top_one, axes, first)
    top_two = lax.ppermute(top_two, axes, second)
    one = lax.ppermute(one, axes, first)
    two = lax.ppermute(two, axes, second)
    star0, total, outgoing = remap(
        top_one, top_two, state, tile_ops[0], edge_local, halo, edge_coef, remap_src.reshape(remaps),
        remap_owner, remap_tile, remap_weight[0], group,
    )
    arrived = lax.all_to_all(
        outgoing.reshape(group, 1, CHUNK * LANES), axes, split_axis=0, concat_axis=0, tiled=True
    )
    base, gain, token = column_part(
        one, two, edge_local, halo, edge_coef, state, tile_ops[0], total, star0, kappa, count
    )
    arrived = lax.ppermute(after(arrived, token), "comp", [(0, 1), (1, 0)])
    return finish(base, gain, arrived.reshape(group * CHUNK, LANES), count)


def solution(mesh):
    placed = (
        P("comp", None, None, ("blk", "sub")),
        P("comp", ("blk", "sub"), None, None),
        P("comp", None, ("blk", "sub")),
        P("comp", ("blk", "sub")),
        P("comp", ("blk", "sub")),
        P("comp", ("blk", "sub")),
        P("comp", ("blk", "sub")),
        P("comp", ("blk", "sub")),
        P("comp", ("blk", "sub"), None),
        P("comp", ("blk", "sub")),
        P("comp", ("blk", "sub"), None, None),
    )
    return jax.shard_map(
        local,
        mesh=mesh,
        in_specs=placed,
        out_specs=(P("comp", None, None, ("blk", "sub")), P("comp", None, ("blk", "sub"))),
        check_vma=False,
    )
```

```python
import jax
import jax.numpy as jnp
from jax import lax
from jax.experimental import pallas as pl
from jax.experimental.pallas import tpu as pltpu
from jax.sharding import PartitionSpec as P

HALO_W = 512
LANES = 128
STEP = 0.25
RELAX = 0.5
CHUNK = 9
F32 = jnp.float32
BF16 = jnp.bfloat16
VMEM = pltpu.VMEM
SMEM = pltpu.SMEM


def split3(x):
    hi = x.astype(BF16)
    rest = x - hi.astype(F32)
    mid = rest.astype(BF16)
    low = (rest - mid.astype(F32)).astype(BF16)
    return hi, mid, low


def split2(x):
    hi = x.astype(BF16)
    return hi, (x - hi.astype(F32)).astype(BF16)


def mm(a, b):
    return jnp.dot(a, b, preferred_element_type=F32)


def vspec():
    return pl.BlockSpec(memory_space=VMEM)


def sspec():
    return pl.BlockSpec(memory_space=SMEM)


def hbm(x):
    return pltpu.with_memory_space_constraint(x, pltpu.HBM)


def aspec():
    return pl.BlockSpec(memory_space=pltpu.HBM)


def params(mib):
    return pltpu.CompilerParams(vmem_limit_bytes=mib * 1024 * 1024)


def sides(even_ref, columns):
    even = even_ref[0] == 1
    last = columns - HALO_W
    return [pl.multiple_of(jnp.where(even, *pair), LANES) for pair in ((last, 0), (0, last))]


def pack_body(even_ref, state_ref, top_one, top_two, one_ref, two_ref, sem):
    loads = [
        pltpu.make_async_copy(state_ref.at[0, :, :, pl.ds(at, HALO_W)], ref, sem.at[i])
        for i, (at, ref) in enumerate(zip(sides(even_ref, state_ref.shape[3]), (one_ref, two_ref)))
    ]
    for load in loads:
        load.start()
    for load, ref, top in zip(loads, (one_ref, two_ref), (top_one, top_two)):
        load.wait()
        top[...] = ref[:, 0, :]


def pack(even, state):
    _, fields, levels, _ = state.shape
    shape = jax.ShapeDtypeStruct
    return pl.pallas_call(
        pack_body,
        in_specs=[sspec(), aspec()],
        out_specs=[vspec()] * 4,
        out_shape=[shape((fields, HALO_W), F32)] * 2 + [shape((fields, levels, HALO_W), F32)] * 2,
        scratch_shapes=[pltpu.SemaphoreType.DMA((2,))],
        cost_estimate=pl.CostEstimate(flops=6 * 10**10, bytes_accessed=3 * 10**6, transcendentals=0),
    )(even, hbm(state))


def gather_halo(pick, index, coef):
    rows = pick(0).shape[0]
    lane = jnp.broadcast_to(jnp.bitwise_and(index, LANES - 1), (rows, LANES))
    part = jnp.broadcast_to(jnp.right_shift(index, 7), (rows, LANES))
    found = jnp.zeros((rows, LANES), F32)
    for h in range(2 * HALO_W // LANES):
        got = jnp.take_along_axis(pick(h), lane, axis=1)
        found = jnp.where(part == h, got, found)
    return found * coef


def rows_of(ref):
    return jnp.concatenate([ref[block : block + 1, :] for block in range(ref.shape[0])], axis=1)


def remap_body(
    one_ref, two_ref, state_ref, ops_ref, local_ref, halo_ref, coef_ref, src_ref, owner_ref, tile_ref, weight_ref,
    star_ref, total_ref, out_ref, window, weights, first_s, second_s, pairs, products, sem,
):
    fields, columns = star_ref.shape
    tiles = columns // LANES
    remaps = weight_ref.shape[0]
    group = out_ref.shape[0] // CHUNK
    parts = 4
    size = remaps // parts
    copies = [
        pltpu.make_async_copy(weight_ref.at[pl.ds(i * size, size)], weights.at[pl.ds(i * size, size)], sem.at[i])
        for i in range(parts)
    ]
    load = pltpu.make_async_copy(state_ref.at[0, :, pl.ds(0, 8), :], window, sem.at[parts])
    load.start()
    for copy in copies:
        copy.start()

    per = HALO_W // LANES

    def pick(h):
        ref = one_ref if h < per else two_ref
        h = h % per
        return ref[:, h * LANES : (h + 1) * LANES]

    blocks = halo_ref.shape[0]
    flow = jnp.concatenate(
        [gather_halo(pick, halo_ref[k : k + 1, :], coef_ref[k : k + 1, :]) for k in range(blocks)], axis=1
    )
    coef = rows_of(coef_ref)
    own = rows_of(local_ref)
    own_tile = jnp.right_shift(own, 7)
    stack = jnp.concatenate([flow, coef], axis=0)
    wide = jnp.concatenate([jnp.where(own_tile == t, stack, 0.0) for t in range(tiles)], axis=0)
    across = jnp.transpose(jnp.bitwise_and(local_ref[...], LANES - 1))
    lane = lax.broadcasted_iota(jnp.int32, (LANES, LANES), 1)
    hot = jnp.concatenate(
        [
            jnp.where(jnp.broadcast_to(across[:, k : k + 1], (LANES, LANES)) == lane, 1.0, 0.0).astype(BF16)
            for k in range(blocks)
        ],
        axis=0,
    )
    spread = sum(mm(part, hot) for part in split3(wide))
    load.wait()
    for tile in range(tiles):
        where = slice(tile * LANES, (tile + 1) * LANES)
        here = window[:, 0, where]
        both = jnp.concatenate(split2(ops_ref[tile]), axis=1)
        mixed = mm(jnp.concatenate(split2(here), axis=1), jnp.concatenate([both, both], axis=0))
        mixed = mixed[:, :LANES] + mixed[:, LANES:]
        base = tile * (fields + 1)
        total = spread[base + fields : base + fields + 1]
        total_ref[:, where] = jnp.broadcast_to(total, (total_ref.shape[0], LANES))
        star = here + STEP * (mixed + (spread[base : base + fields] - total * here))
        star_ref[:, where] = star
        surface = star.astype(BF16).astype(F32)
        nothing = jnp.zeros_like(surface)
        first_s[tile] = jnp.concatenate([surface, nothing], axis=0)
        second_s[tile] = jnp.concatenate([nothing, surface], axis=0)
    for pair in range(remaps // 2):
        left = first_s[src_ref[2 * pair]]
        right = second_s[src_ref[2 * pair + 1]]
        pairs[pair] = jnp.concatenate([left, right], axis=1)
    for part in range(parts):
        copies[part].wait()
        for pair in range(part * size // 2, (part + 1) * size // 2):
            weight = weights[2 * pair : 2 * pair + 2].reshape(2 * LANES, LANES)
            products[2 * fields * pair : 2 * fields * (pair + 1)] = mm(pairs[pair].astype(BF16), weight)

    owner = owner_ref[...]
    down = lax.broadcasted_iota(jnp.int32, (remaps, remaps), 0)
    right = lax.broadcasted_iota(jnp.int32, (remaps, remaps), 1)
    owner_rows = jnp.broadcast_to(owner, (remaps, remaps))
    owner_columns = jnp.transpose(owner_rows)
    earlier = jnp.where((owner_rows == owner_columns) & (down < right), 1, 0)
    rank = jnp.sum(earlier, axis=0, keepdims=True)
    dest = lax.broadcasted_iota(jnp.int32, (group, remaps), 0)
    named = jnp.broadcast_to(owner, (group, remaps)) == dest
    slots = [named & (jnp.broadcast_to(rank, (group, remaps)) == k) for k in range(2)]
    place = jnp.concatenate([jnp.where(slot, 1.0, 0.0).astype(BF16) for slot in slots], axis=0)
    wanted = tile_ref[...]
    labels = [jnp.max(jnp.where(slot, wanted, -1), axis=1, keepdims=True) for slot in slots]
    side = lax.broadcasted_iota(jnp.int32, (group, LANES), 1)
    note = jnp.where(side == 0, labels[0], jnp.where(side == 1, labels[1], -1))
    out_ref[pl.ds(2 * fields, group, stride=CHUNK), :] = note.astype(F32)
    for field in range(fields):
        value = products[pl.ds(field, remaps, stride=fields), :]
        placed = sum(mm(place, part) for part in split3(value))
        for k in range(2):
            out_ref[pl.ds(k * fields + field, group, stride=CHUNK), :] = placed[k * group : (k + 1) * group]


def remap(one, two, state, ops, edge_local, edge_halo, edge_coef, src, owners, wanted, weight, group):
    _, fields, _, columns = state.shape
    remaps = weight.shape[0]
    blocks = edge_halo.size // LANES
    tiles = columns // LANES
    fold = lambda x: x.reshape(blocks, LANES)
    return pl.pallas_call(
        remap_body,
        in_specs=[vspec()] * 2 + [aspec()] + [vspec()] * 4 + [sspec(), vspec(), vspec(), aspec()],
        out_specs=[vspec()] * 3,
        out_shape=[
            jax.ShapeDtypeStruct((fields, columns), F32),
            jax.ShapeDtypeStruct((8, columns), F32),
            jax.ShapeDtypeStruct((group * CHUNK, LANES), F32),
        ],
        scratch_shapes=[
            pltpu.VMEM((fields, 8, columns), F32),
            pltpu.VMEM(weight.shape, BF16),
            pltpu.VMEM((tiles, 2 * fields, LANES), F32),
            pltpu.VMEM((tiles, 2 * fields, LANES), F32),
            pltpu.VMEM((remaps // 2, 2 * fields, 2 * LANES), F32),
            pltpu.VMEM((remaps * fields, LANES), F32),
            pltpu.SemaphoreType.DMA((5,)),
        ],
        compiler_params=params(16),
        cost_estimate=pl.CostEstimate(flops=6 * 10**10, bytes_accessed=6 * 10**6, transcendentals=0),
    )(
        one, two, hbm(state), ops, fold(edge_local), fold(edge_halo), fold(edge_coef), src,
        owners.reshape(1, remaps), wanted.reshape(1, remaps), hbm(weight),
    )


def column_body(
    one_ref, two_ref, local_ref, halo_ref, coef_ref, state_ref, ops_ref, total_ref, star_ref, kappa_ref,
    active_ref, base_ref, gain_ref, token_ref, flow_hi, flow_lo, work, inv, up, down,
):
    step = pl.program_id(0)
    token_ref[...] = jnp.zeros_like(token_ref)
    _, fields, levels, width = state_ref.shape
    rows = fields * levels
    per = HALO_W // LANES
    blocks = halo_ref.shape[0]
    tiles = range(width // LANES)
    cut = [slice(tile * LANES, (tile + 1) * LANES) for tile in tiles]

    @pl.when(step == 0)
    def _():
        def pick(h):
            where = slice((h % per) * LANES, (h % per + 1) * LANES)
            ref = one_ref if h < per else two_ref
            return ref[:, :, where].reshape(rows, LANES)

        down_h = lax.broadcasted_iota(jnp.int32, (2 * HALO_W, LANES), 0)
        parts = split2(jnp.concatenate([pick(h) for h in range(2 * per)], axis=1))
        for k in range(0, blocks, 2):
            rows_k = [slice(k + j, k + j + 1) for j in range(2)]
            here = [jnp.where(down_h == halo_ref[row, :], 1.0, 0.0).astype(BF16) for row in rows_k]
            here = jnp.concatenate(here, axis=1)
            coef = jnp.concatenate([coef_ref[row, :] for row in rows_k], axis=1)
            hi, lo = split2((mm(parts[0], here) + mm(parts[1], here)) * coef)
            flow_hi[:, k * LANES : (k + 2) * LANES] = hi
            flow_lo[:, k * LANES : (k + 2) * LANES] = lo

    across = jnp.transpose(local_ref[...] - step * width)
    lane = lax.broadcasted_iota(jnp.int32, (LANES, LANES), 1)
    hot = []
    for k in range(blocks):
        own = jnp.broadcast_to(across[:, k : k + 1], (LANES, LANES)) - lane
        hot.append(jnp.concatenate([jnp.where(own == t * LANES, 1.0, 0.0).astype(BF16) for t in tiles], axis=1))
    hot = jnp.concatenate(hot, axis=0)
    extra = mm(flow_hi[...], hot) + mm(flow_lo[...], hot)
    for tile in tiles:
        here = state_ref[0, :, :, cut[tile]].reshape(rows, LANES)
        both = jnp.concatenate(split2(ops_ref[tile]), axis=1)
        mixed = mm(jnp.concatenate(split2(here), axis=1), jnp.concatenate([both, both], axis=0))
        mixed = mixed[:, :LANES] + mixed[:, LANES:]
        work[tile] = here + STEP * ((mixed - here * total_ref[0:1, cut[tile]]) + extra[:, cut[tile]])

    depth = lax.broadcasted_iota(jnp.int32, (levels, LANES), 0)
    for tile in tiles:
        count = active_ref[step * len(tiles) + tile]
        down[:, cut[tile]] = jnp.where(depth + 1 < count, -STEP * kappa_ref[0, :, cut[tile]], 0.0)
    last = levels - 1
    upper = down[last : last + 1, :]
    lower = down[last - 1 : last, :]
    inverse = 1.0 / (1.0 - lower - upper)
    ratio = lower * inverse
    inv[last : last + 1, :] = inverse
    up[last : last + 1, :] = upper * inverse
    down[last : last + 1, :] = ratio
    for level in range(last - 1, -1, -1):
        row = slice(level, level + 1)
        upper = lower
        lower = down[level - 1 : level, :] if level else jnp.zeros_like(upper)
        inverse = 1.0 / (1.0 - lower - upper - upper * ratio)
        ratio = lower * inverse
        inv[row, :] = inverse
        up[row, :] = upper * inverse
        down[row, :] = ratio
    gain = RELAX * inverse
    gain_ref[0:1, :] = gain
    for level in range(1, levels):
        gain = -gain * down[level : level + 1, :]
        gain_ref[level : level + 1, :] = gain

    values = [None for _ in tiles]
    for level in range(last, -1, -1):
        row = slice(level, level + 1)
        spot = pl.ds(level, fields, stride=levels)
        for tile in tiles:
            rhs = work[tile, spot, :] if level else RELAX * star_ref[:, cut[tile]]
            scaled = rhs * inv[row, cut[tile]]
            value = values[tile]
            values[tile] = scaled if value is None else scaled - up[row, cut[tile]] * value
            work[tile, spot, :] = values[tile]
    for level in range(1, levels):
        row = slice(level, level + 1)
        spot = pl.ds(level, fields, stride=levels)
        for tile in tiles:
            values[tile] = work[tile, spot, :] - down[row, cut[tile]] * values[tile]
            work[tile, spot, :] = values[tile]
    for tile in tiles:
        base_ref[:, :, cut[tile]] = work[tile].reshape(fields, levels, LANES)


def column_part(one, two, edge_local, edge_halo, edge_coef, state, ops, total, star, kappa, active):
    _, fields, levels, columns = state.shape
    steps = 4
    width = columns // steps
    edges = edge_halo.size
    blocks = edges // LANES
    column = pl.BlockSpec((levels, width), lambda i: (0, i))
    whole = lambda x: pl.BlockSpec(x.shape, lambda i: (0,) * x.ndim)
    lists = [x.reshape(blocks, LANES) for x in (edge_local, edge_halo, edge_coef)]
    return pl.pallas_call(
        column_body,
        grid=(steps,),
        in_specs=[whole(x) for x in (one, two, *lists)]
        + [
            pl.BlockSpec((1, fields, levels, width), lambda i: (0, 0, 0, i)),
            pl.BlockSpec((width // LANES, LANES, LANES), lambda i: (i, 0, 0)),
            pl.BlockSpec((8, width), lambda i: (0, i)),
            pl.BlockSpec((fields, width), lambda i: (0, i)),
            pl.BlockSpec((1, levels, width), lambda i: (0, 0, i)),
            sspec(),
        ],
        out_specs=[
            pl.BlockSpec((fields, levels, width), lambda i: (0, 0, i)),
            column,
            pl.BlockSpec((8, LANES), lambda i: (0, 0)),
        ],
        out_shape=[
            jax.ShapeDtypeStruct((fields, levels, columns), F32),
            jax.ShapeDtypeStruct((levels, columns), F32),
            pltpu.HBM((8, LANES), F32),
        ],
        scratch_shapes=[
            pltpu.VMEM((fields * levels, edges), BF16),
            pltpu.VMEM((fields * levels, edges), BF16),
            pltpu.VMEM((width // LANES, fields * levels, LANES), F32),
            pltpu.VMEM((levels, width), F32),
            pltpu.VMEM((levels, width), F32),
            pltpu.VMEM((levels, width), F32),
        ],
        compiler_params=params(24),
        cost_estimate=pl.CostEstimate(flops=6 * 10**10, bytes_accessed=10**7, transcendentals=0),
    )(hbm(one), hbm(two), *lists, hbm(state), hbm(ops), total, star, hbm(kappa), active)


def finish_body(base_ref, gain_ref, arrived_ref, active_ref, out_ref, flux_out, flux_ref, result, sem):
    fields, levels, columns = base_ref.shape
    steps = result.shape[0]
    width = columns // steps
    stores = [
        pltpu.make_async_copy(result.at[i], out_ref.at[0, :, :, pl.ds(i * width, width)], sem.at[i])
        for i in range(steps)
    ]
    tiles = columns // LANES
    sources = arrived_ref.shape[0] // CHUNK
    labels = jnp.transpose(arrived_ref[pl.ds(2 * fields, sources, stride=CHUNK), :])
    named = lax.broadcasted_iota(jnp.int32, (tiles, sources), 0).astype(F32)
    select = jnp.concatenate(
        [jnp.where(named == labels[k : k + 1, :], 1.0, 0.0).astype(BF16) for k in range(2)], axis=1
    )
    for field in range(fields):
        value = jnp.concatenate(
            [arrived_ref[pl.ds(k * fields + field, sources, stride=CHUNK), :] for k in range(2)], axis=0
        )
        flux_ref[field] = sum(mm(select, part) for part in split3(value))
    depth = lax.broadcasted_iota(jnp.int32, (levels, LANES), 0)
    for i in range(steps):
        for tile in range(width // LANES):
            place = i * (width // LANES) + tile
            whole = slice(place * LANES, (place + 1) * LANES)
            where = slice(tile * LANES, (tile + 1) * LANES)
            inside = depth < active_ref[place]
            gain = gain_ref[:, whole]
            for field in range(fields):
                flux = flux_ref[field, place : place + 1, :]
                flux_out[0, field : field + 1, whole] = flux
                result[i, field, :, where] = jnp.where(inside, base_ref[field, :, whole] + gain * flux, 0.0)
        stores[i].start()
    for store in stores:
        store.wait()


def finish(base, gain, arrived, active):
    fields, levels, columns = base.shape
    steps = 4
    return pl.pallas_call(
        finish_body,
        in_specs=[vspec(), vspec(), vspec(), sspec()],
        out_specs=[aspec(), vspec()],
        out_shape=[
            jax.ShapeDtypeStruct((1, fields, levels, columns), F32),
            jax.ShapeDtypeStruct((1, fields, columns), F32),
        ],
        scratch_shapes=[
            pltpu.VMEM((fields, columns // LANES, LANES), F32),
            pltpu.VMEM((steps, fields, levels, columns // steps), F32),
            pltpu.SemaphoreType.DMA((steps,)),
        ],
        compiler_params=params(16),
        cost_estimate=pl.CostEstimate(flops=10**7, bytes_accessed=6 * 10**6, transcendentals=0),
    )(base, gain, arrived, active)


def after_body(value_ref, token_ref, out_ref):
    pass


def after(value, token):
    anywhere = pl.BlockSpec(memory_space=pl.ANY)
    return pl.pallas_call(
        after_body,
        in_specs=[anywhere, anywhere],
        out_specs=anywhere,
        out_shape=jax.ShapeDtypeStruct(value.shape, value.dtype),
        input_output_aliases={0: 0},
        cost_estimate=pl.CostEstimate(flops=0, bytes_accessed=0, transcendentals=0),
    )(value, token)


def local(
    state, tile_ops, kappa, active, edge_local, edge_halo, edge_coef, remap_src, remap_owner, remap_tile, remap_weight
):
    _, fields, levels, columns = state.shape
    tiles = tile_ops.shape[1]
    remaps = remap_src.shape[1]
    axes = ("blk", "sub")
    group = lax.axis_size("blk") * lax.axis_size("sub")
    first = [(i, i ^ 1) for i in range(group)]
    second = [(i, (i + 1) % group if i % 2 else (i - 1) % group) for i in range(group)]
    even = (1 - lax.axis_index("sub") % 2).astype(jnp.int32).reshape(1)
    count = active.reshape(tiles)
    halo = jnp.bitwise_xor(edge_halo, HALO_W * even[0])

    top_one, top_two, one, two = pack(even, state)
    top_one = lax.ppermute(top_one, axes, first)
    top_two = lax.ppermute(top_two, axes, second)
    one = lax.ppermute(one, axes, first)
    two = lax.ppermute(two, axes, second)
    star0, total, outgoing = remap(
        top_one, top_two, state, tile_ops[0], edge_local, halo, edge_coef, remap_src.reshape(remaps),
        remap_owner, remap_tile, remap_weight[0], group,
    )
    arrived = lax.all_to_all(
        outgoing.reshape(group, 1, CHUNK * LANES), axes, split_axis=0, concat_axis=0, tiled=True
    )
    base, gain, token = column_part(
        one, two, edge_local, halo, edge_coef, state, tile_ops[0], total, star0, kappa, count
    )
    arrived = lax.ppermute(after(arrived, token), "comp", [(0, 1), (1, 0)])
    return finish(base, gain, arrived.reshape(group * CHUNK, LANES), count)


def solution(mesh):
    placed = (
        P("comp", None, None, ("blk", "sub")),
        P("comp", ("blk", "sub"), None, None),
        P("comp", None, ("blk", "sub")),
        P("comp", ("blk", "sub")),
        P("comp", ("blk", "sub")),
        P("comp", ("blk", "sub")),
        P("comp", ("blk", "sub")),
        P("comp", ("blk", "sub")),
        P("comp", ("blk", "sub"), None),
        P("comp", ("blk", "sub")),
        P("comp", ("blk", "sub"), None, None),
    )
    return jax.shard_map(
        local,
        mesh=mesh,
        in_specs=placed,
        out_specs=(P("comp", None, None, ("blk", "sub")), P("comp", None, ("blk", "sub"))),
        check_vma=False,
    )
```
